32 devices in a mesh: groups: 2 (over x), tracks: 8 (over z, y), frames: 2 (over core).
Axes of the slice: x: 2, y: 2, z: 4, core: 2. Of those that a mesh axis runs over, the one named last changes fastest.
Arguments:
- tokens: bfloat16 [256, 256, 384], P(('groups', 'tracks'), 'frames'), parts along dimension 0, may hold values from -6 to 6
- first_frame: int32 [256], P(('groups', 'tracks')), parts along dimension 0, may hold values from 0 to 127
- visible: int32 [256, 256], P(('groups', 'tracks')), parts along dimension 0, may hold values 0 or 1
- time_qkv: bfloat16 [384, 1152], replicated, may hold values from -0.3125 to 0.3125
- time_output: bfloat16 [384, 384], replicated, may hold values from -0.3125 to 0.3125
- expand: bfloat16 [384, 1536], replicated, may hold values from -0.3125 to 0.3125
- shrink: bfloat16 [1536, 384], replicated, may hold values from -0.15625 to 0.15625
- virtual_init: bfloat16 [64, 384], replicated, may hold values from -6 to 6
- cross_query: bfloat16 [384, 384], replicated, may hold values from -0.3125 to 0.3125
- cross_kv: bfloat16 [384, 768], replicated, may hold values from -0.3125 to 0.3125
- cross_output: bfloat16 [384, 384], replicated, may hold values from -1.25 to 1.25
- self_qkv: bfloat16 [384, 1152], replicated, may hold values from -0.3125 to 0.3125
- self_output: bfloat16 [384, 384], replicated, may hold values from -0.625 to 0.625
- back_query: bfloat16 [384, 384], replicated, may hold values from -0.3125 to 0.3125
- back_kv: bfloat16 [384, 768], replicated, may hold values from -0.3125 to 0.3125
- back_output: bfloat16 [384, 384], replicated, may hold values from -1.25 to 1.25
Outputs:
- tracked: bfloat16 [256, 256, 384], P(('groups', 'tracks'), 'frames'), parts along dimension 0
The draws below stay inside these ranges and needn't reach their ends.
There are 2 independent parts, one for each index of `groups`. The reference program is written for one: setup_inputs(seed, part) draws one part's arguments, and reference() takes and returns one part's arrays. A program takes and returns all parts, laid end to end along the dimension named above; an argument that names none is the same for every part. Nothing has to cross between parts.
Inputs may be any that keep to these rules, and one draw needn't show every extreme that they name: `first_frame`: each track's first frame.
All inputs are finite; a program needn't handle non-finite values. No bound on the sum of `visible` on one device may be relied on, other than what follows from the above.
Results may differ from the reference program's by a relative error of at most 0.0095.
Values may be sent and summed in bfloat16 or wider, within the bound.
No kernel may reach another device: no remote copies, remote signals or barrier semaphores. Data moves between devices by JAX's collectives and lax.ppermute only.
A program may use at most 128 MiB of HBM per device.

```python
import jax
import jax.numpy as jnp
from jax import lax

D = 384
FF = 1536
HEADS = 8
VIRT = 64
HEAD = 48
TRK_DEV = 16
FRM_DEV = 128
TRACKS = 128
FRAMES = 256
N_TRACKS = 8
N_FRAMES = 2


def touch_ends(drawn, rng, smallest, high):
    spot = [jax.random.randint(jax.random.fold_in(rng, axis), (), 0, length) for axis, length in enumerate(drawn.shape)]
    main_axis = drawn.shape.index(max(drawn.shape))
    next_to = spot[:main_axis] + [(spot[main_axis] + 1) % drawn.shape[main_axis]] + spot[main_axis + 1:]
    return drawn.at[tuple(spot)].set(smallest).at[tuple(next_to)].set(high)


def steps_of(stream_key, shape, cuts, smallest, high):
    def one(dim, shards_of):
        steps = jax.random.uniform(jax.random.fold_in(jax.random.fold_in(stream_key, 6), dim), (shards_of,), jnp.float32, smallest / len(cuts), high / len(cuts))
        return jnp.repeat(jnp.exp(steps), shape[dim] // shards_of).reshape((-1,) + (1,) * (len(shape) - dim - 1))

    level = one(*cuts[0])
    for cut in cuts[1:]:
        level = level * one(*cut)
    return level


def gaussian(stream_key, dims, width, most, cuts=(), kind=jnp.bfloat16):
    factor_of = steps_of(stream_key, dims, cuts, -0.22, 0.18) if cuts else 1.0
    array = jax.random.normal(stream_key, dims, jnp.float32) * width * factor_of
    return jnp.minimum(jnp.maximum(array, -most), most).astype(kind)


def setup_inputs(seed: int = 0, part: int = 0) -> dict:
    keys = jax.random.split(jax.random.key(seed), 17)
    own_keys = jax.random.split(jax.random.fold_in(keys[16], part), 17)
    tokens = gaussian(own_keys[0], (TRACKS, FRAMES, D), 1.0, 6.0, ((0, 8), (1, 2)))
    first_frame = touch_ends(jax.random.randint(own_keys[1], (TRACKS,), 0, FRAMES // 2), jax.random.fold_in(own_keys[1], 1), 0, (FRAMES // 2) - 1).astype(jnp.int32)
    visible = touch_ends((jax.random.randint(own_keys[2], (TRACKS, FRAMES), 0, 4) < 3).astype(jnp.int32), jax.random.fold_in(own_keys[2], 1), 0, 1)
    time_qkv = gaussian(keys[3], (D, 3 * D), D ** -0.5, 0.3125)
    time_output = gaussian(keys[4], (D, D), D ** -0.5, 0.3125)
    expand = gaussian(keys[5], (D, FF), D ** -0.5, 0.3125)
    shrink = gaussian(keys[6], (FF, D), FF ** -0.5, 0.15625)
    virtual_init = gaussian(keys[7], (VIRT, D), 1.0, 6.0)
    cross_query = gaussian(keys[8], (D, D), D ** -0.5, 0.3125)
    cross_kv = gaussian(keys[9], (D, 2 * D), D ** -0.5, 0.3125)
    cross_output = gaussian(keys[10], (D, D), (D // 16) ** -0.5, 1.25)
    self_qkv = gaussian(keys[11], (D, 3 * D), D ** -0.5, 0.3125)
    self_output = gaussian(keys[12], (D, D), (D // 4) ** -0.5, 0.625)
    back_query = gaussian(keys[13], (D, D), D ** -0.5, 0.3125)
    back_kv = gaussian(keys[14], (D, 2 * D), D ** -0.5, 0.3125)
    back_output = gaussian(keys[15], (D, D), (D // 16) ** -0.5, 1.25)
    return {"tokens": tokens, "first_frame": first_frame, "visible": visible, "time_qkv": time_qkv, "time_output": time_output, "expand": expand, "shrink": shrink, "virtual_init": virtual_init, "cross_query": cross_query, "cross_kv": cross_kv, "cross_output": cross_output, "self_qkv": self_qkv, "self_output": self_output, "back_query": back_query, "back_kv": back_kv, "back_output": back_output}


def normed(values):
    values = values.astype(jnp.float32)
    return values * lax.rsqrt(lax.optimization_barrier(jnp.mean(values * values, axis=-1, keepdims=True)) + 1e-06)

def product(pattern, first_operand, second_operand):
    return jnp.einsum(pattern, first_operand.astype(jnp.float32), second_operand.astype(jnp.float32))

def split_heads(values):
    return values.reshape(values.shape[:-1] + (HEADS, HEAD))

def merge_heads(values):
    return values.reshape(values.shape[:-2] + (D,))

def usable_keys(first_frame, visible, offset, length):
    frames = offset + jnp.arange(length, dtype=jnp.int32)
    seen = lax.dynamic_slice_in_dim(visible, offset, length, 1)
    return (frames[None, :] >= first_frame[:, None]) & ((seen == 1) | (frames[None, :] == first_frame[:, None]))

def time_project(tokens, time_qkv):
    projected = product('ntd,dk->ntk', normed(tokens).astype(jnp.bfloat16), time_qkv)
    time_query = normed(projected[..., :D]).astype(jnp.bfloat16)
    time_key = normed(projected[..., D:2 * D]).astype(jnp.bfloat16)
    time_value = projected[..., 2 * D:].astype(jnp.bfloat16)
    return (time_query, time_key, time_value)

def time_terms(time_query, key_piece, value_piece, usable):
    scores = product('nqhe,nkhe->nhqk', split_heads(time_query), split_heads(key_piece)) * HEAD ** (-0.5)
    weights = (jnp.exp(scores) * usable[:, None, None, :].astype(jnp.float32)).astype(jnp.bfloat16)
    numerator = product('nhqk,nkhe->nqhe', weights, split_heads(value_piece))
    denominator = jnp.transpose(lax.optimization_barrier(jnp.sum(weights.astype(jnp.float32), axis=-1)), (0, 2, 1))
    return (numerator, denominator)

def time_finish(tokens, numerator, denominator, time_output, expand, shrink):
    time_mixed = merge_heads(numerator / denominator[..., None]).astype(jnp.bfloat16)
    middle = tokens.astype(jnp.float32) + product('ntd,dk->ntk', time_mixed, time_output)
    middle_norm = normed(middle).astype(jnp.bfloat16)
    hidden = jax.nn.gelu(product('ntd,df->ntf', middle_norm, expand), approximate=True).astype(jnp.bfloat16)
    return (middle + product('ntf,fd->ntd', hidden, shrink)).astype(jnp.bfloat16)

def attend_pair(query, key, value, query_form, value_form):
    weights = jnp.exp(product(query_form, split_heads(query), split_heads(key)) * HEAD ** (-0.5)).astype(jnp.bfloat16)
    numerator = product(value_form, weights, split_heads(value))
    return (weights, numerator)

def virtual_block(settled, virtual_init, cross_query, cross_kv, cross_output, self_qkv, self_output, back_query, back_kv, back_output):
    settled_norm = normed(settled).astype(jnp.bfloat16)
    crossed = product('nfd,dk->nfk', settled_norm, cross_kv)
    track_key = normed(crossed[..., :D]).astype(jnp.bfloat16)
    track_value = crossed[..., D:].astype(jnp.bfloat16)
    virtual_norm = normed(virtual_init).astype(jnp.bfloat16)
    virtual_query = normed(product('jd,dk->jk', virtual_norm, cross_query)).astype(jnp.bfloat16)
    cross_weight, numerator = attend_pair(virtual_query, track_key, track_value, 'jhe,nfhe->fhjn', 'fhjn,nfhe->fjhe')
    totals = jnp.transpose(lax.optimization_barrier(jnp.sum(cross_weight.astype(jnp.float32), axis=-1)), (0, 2, 1))
    cross_mixed = merge_heads(numerator / totals[..., None]).astype(jnp.bfloat16)
    virtual_first = virtual_init.astype(jnp.float32)[None] + product('fjd,dk->fjk', cross_mixed, cross_output)
    selfed = product('fjd,dk->fjk', normed(virtual_first).astype(jnp.bfloat16), self_qkv)
    self_query = normed(selfed[..., :D]).astype(jnp.bfloat16)
    self_key = normed(selfed[..., D:2 * D]).astype(jnp.bfloat16)
    self_value = selfed[..., 2 * D:].astype(jnp.bfloat16)
    self_weight, numerator = attend_pair(self_query, self_key, self_value, 'fjhe,fihe->fhji', 'fhji,fihe->fjhe')
    totals = jnp.transpose(lax.optimization_barrier(jnp.sum(self_weight.astype(jnp.float32), axis=-1)), (0, 2, 1))
    self_mixed = merge_heads(numerator / totals[..., None]).astype(jnp.bfloat16)
    virtual_second = virtual_first + product('fjd,dk->fjk', self_mixed, self_output)
    backed = product('fjd,dk->fjk', normed(virtual_second).astype(jnp.bfloat16), back_kv)
    virtual_key = normed(backed[..., :D]).astype(jnp.bfloat16)
    virtual_value = backed[..., D:].astype(jnp.bfloat16)
    track_query = normed(product('nfd,dk->nfk', settled_norm, back_query)).astype(jnp.bfloat16)
    back_weight, numerator = attend_pair(track_query, virtual_key, virtual_value, 'nfhe,fjhe->nfhj', 'nfhj,fjhe->nfhe')
    totals = lax.optimization_barrier(jnp.sum(back_weight.astype(jnp.float32), axis=-1))
    back_mixed = merge_heads(numerator / totals[..., None]).astype(jnp.bfloat16)
    return (settled.astype(jnp.float32) + product('nfd,dk->nfk', back_mixed, back_output)).astype(jnp.bfloat16)

def reference(tokens, first_frame, visible, time_qkv, time_output, expand, shrink, virtual_init, cross_query, cross_kv, cross_output, self_qkv, self_output, back_query, back_kv, back_output):
    track_block = TRK_DEV // N_FRAMES
    blocks = TRACKS // track_block

    def time_part(grouped):
        time_query, time_key, time_value = time_project(grouped[0], time_qkv)
        usable = usable_keys(grouped[1], grouped[2], 0, FRAMES)
        numerator, denominator = time_terms(time_query, time_key, time_value, usable)
        return time_finish(grouped[0], numerator, denominator, time_output, expand, shrink)
    settled = lax.map(time_part, (tokens.reshape(blocks, track_block, FRAMES, D), first_frame.reshape(blocks, track_block), visible.reshape(blocks, track_block, FRAMES)))
    settled = settled.reshape(TRACKS, FRAMES, D)
    frame_block = FRM_DEV // N_TRACKS
    pieces = jnp.transpose(settled.reshape(TRACKS, FRAMES // frame_block, frame_block, D), (1, 0, 2, 3))

    def virtual_part(section):
        return virtual_block(section, virtual_init, cross_query, cross_kv, cross_output, self_qkv, self_output, back_query, back_kv, back_output)
    tracked = lax.map(virtual_part, pieces)
    return jnp.transpose(tracked, (1, 0, 2, 3)).reshape(TRACKS, FRAMES, D)
```

```python
import functools

import jax
import jax.numpy as jnp
from jax import lax
from jax.experimental import pallas as pl
from jax.experimental.pallas import tpu as pltpu
from jax.sharding import PartitionSpec as P

HEADS = 8
EPS = 1e-06
BF = jnp.bfloat16
F32 = jnp.float32


def dot(a, b):
    return lax.dot_general(a, b, (((1,), (0,)), ((), ())), preferred_element_type=F32)


def dot_t(a, b):
    return lax.dot_general(a, b, (((1,), (1,)), ((), ())), preferred_element_type=F32)


def normed(x, scale=None):
    r = lax.rsqrt(jnp.mean(x * x, axis=-1, keepdims=True) + EPS)
    return x * (r if scale is None else r * scale)


def gelu(x):
    c = 0.7978845608028654
    h = 0.5 * x
    return h + h * jnp.tanh(x * (c + (c * 0.044715) * (x * x)))


def windows(d):
    head = d // HEADS
    half = HEADS // 2
    width = -(-half * head // 128) * 128
    last = d - width
    return (
        (0, width, [h * head for h in range(half)]),
        (last, width, [h * head - last for h in range(half, HEADS)]),
    )


def head_mask(rows, width, start, head):
    lane = lax.broadcasted_iota(jnp.int32, (rows, width), 1)
    return jnp.where((lane >= start) & (lane < start + head), 1.0, 0.0).astype(BF)


def merge_windows(low, high, d):
    width = low.shape[1]
    over = 2 * width - d
    pieces = [low[:, : width - over]]
    if over:
        pieces.append(low[:, width - over :] + high[:, :over])
    pieces.append(high[:, over:])
    return jnp.concatenate(pieces, axis=1)


def time_kernel(
    tps, core_ref, first_ref, visible_ref, own_ref, other_ref, qkv_ref, out_w_ref, expand_ref, shrink_ref, out_ref, x_ref
):
    core = core_ref[0]
    base = core_ref[1]
    d = own_ref.shape[-1]
    head = d // HEADS
    tau = head**-0.5
    half = own_ref.shape[1]
    length = 2 * half
    step = pl.program_id(0)
    x_ref[core] = own_ref[...]
    x_ref[1 - core] = other_ref[...]
    wins = windows(d)
    for i in range(tps):
        x = x_ref[:, i].reshape(length, d).astype(F32)
        projected = dot(normed(x).astype(BF), qkv_ref[...])
        query = normed(projected[:, :d], tau).astype(BF)
        key = normed(projected[:, d : 2 * d]).astype(BF)
        value = projected[:, 2 * d :].astype(BF)
        track = base + step * tps + i
        frame = lax.broadcasted_iota(jnp.int32, (1, length), 1)
        first = first_ref[track]
        seen = visible_ref[pl.ds(track, 1), :]
        usable = (frame >= first) & ((seen == 1) | (frame == first))
        usable = jnp.where(usable, 1.0, 0.0)
        usable = jnp.transpose(jnp.broadcast_to(usable, (128, length)), (1, 0)).astype(BF)
        tops, bottoms = [], []
        for first_lane, width, starts in wins:
            q = query[:, first_lane : first_lane + width]
            k = key[:, first_lane : first_lane + width]
            use = jnp.concatenate([usable] * (width // 128), axis=1)
            v = value[:, first_lane : first_lane + width] * use
            masks = [head_mask(length, width, s, head) for s in starts]
            scores = dot_t(jnp.concatenate([q * m for m in masks], axis=0), k)
            weights = jnp.exp(scores).astype(BF)
            weights = jnp.concatenate(
                [weights[h * length : (h + 1) * length] for h in range(len(starts))], axis=1
            )
            tops.append(dot(weights, jnp.concatenate([v * m for m in masks], axis=0)))
            bottoms.append(dot(weights, jnp.concatenate([use * m for m in masks], axis=0)))
        mixed = (merge_windows(*tops, d) / merge_windows(*bottoms, d)).astype(BF)
        middle = x + dot(mixed, out_w_ref[...])
        hidden = gelu(dot(normed(middle).astype(BF), expand_ref[...])).astype(BF)
        settled = (middle + dot(hidden, shrink_ref[...])).astype(BF)
        if len(out_ref.shape) == 5:
            spots, _, _, rows, _ = out_ref.shape
            for c in range(2):
                out_ref[:, c, i] = settled[c * half : (c + 1) * half].reshape(spots, rows, d)
        else:
            out_ref[i] = settled


def full(shape):
    return pl.BlockSpec(shape, lambda *_: (0,) * len(shape))


def time_part(own, other, first_frame, visible, where, weights, spots, tps):
    tracks, half, d = own.shape
    rows = half // spots
    split = rows % 16 == 0
    if split:
        out_shape = (spots, 2, tracks, rows, d)
        out_spec = pl.BlockSpec((spots, 2, tps, rows, d), lambda i, *_: (0, 0, i, 0, 0))
    else:
        out_shape = (tracks, 2 * half, d)
        out_spec = pl.BlockSpec((tps, 2 * half, d), lambda i, *_: (i, 0, 0))
    block = pl.BlockSpec((tps, half, d), lambda i, *_: (i, 0, 0))
    out = pl.pallas_call(
        functools.partial(time_kernel, tps),
        out_shape=jax.ShapeDtypeStruct(out_shape, BF),
        grid_spec=pltpu.PrefetchScalarGridSpec(
            num_scalar_prefetch=2,
            grid=(tracks // tps,),
            in_specs=[full(visible.shape), block, block] + [full(w.shape) for w in weights],
            out_specs=out_spec,
            scratch_shapes=[pltpu.VMEM((2, tps, half, d), BF)],
        ),
        compiler_params=pltpu.CompilerParams(vmem_limit_bytes=48 * 1024 * 1024),
        name="time_part",
    )(where, first_frame, visible, own, other, *weights)
    if not split:
        out = jnp.transpose(out.reshape(tracks, 2, spots, rows, d), (2, 1, 0, 3, 4))
    return out


def regroup(rows, frames, inverse):
    tracks = rows // frames
    r = lax.broadcasted_iota(jnp.int32, (rows, rows), 0)
    c = lax.broadcasted_iota(jnp.int32, (rows, rows), 1)
    if inverse:
        r, c = c, r
    source = (r % tracks) * frames + r // tracks
    return jnp.where(c == source, 1.0, 0.0).astype(BF)


def virtual_kernel(
    frames, block, group,
    x_ref, init_ref, cq_ref, ckv_ref, co_ref, sqkv_ref, so_ref, bq_ref, bkv_ref, bo_ref,
    out_ref, rows_ref,
):
    total, d = x_ref.shape
    head = d // HEADS
    tau = head**-0.5
    tracks = total // frames
    part = group // frames
    virt = init_ref.shape[0]
    wins = windows(d)
    there = regroup(group, frames, False)
    for g in range(total // group):
        moved = dot(there, x_ref[g * group : (g + 1) * group, :]).astype(BF)
        for f in range(frames):
            rows_ref[f * tracks + g * part : f * tracks + (g + 1) * part, :] = moved[f * part : (f + 1) * part]
    init = init_ref[...].astype(F32)
    vq = normed(dot(normed(init).astype(BF), cq_ref[...]), tau).astype(BF)
    n_half = HEADS // 2
    stacked = []
    for first_lane, width, starts in wins:
        q = vq[:, first_lane : first_lane + width]
        stacked.append(jnp.concatenate([q * head_mask(virt, width, s, head) for s in starts], axis=0))
    width = wins[0][1]
    track_masks = [[head_mask(tracks, width, s, head) for s in starts] for _, _, starts in wins]
    virt_masks = [[head_mask(virt, width, s, head) for s in starts] for _, _, starts in wins]
    track_ones = [jnp.concatenate(m, axis=0) for m in track_masks]
    virt_ones = [jnp.concatenate(m, axis=0) for m in virt_masks]

    def virtual_attention(query, key, value):
        tops, weights = [], []
        for w, (first_lane, width, starts) in enumerate(wins):
            lanes = slice(first_lane, first_lane + width)
            k = jnp.concatenate([key[:, lanes] * m for m in virt_masks[w]], axis=0)
            v = jnp.concatenate([value[:, lanes] * m for m in virt_masks[w]], axis=0)
            p = jnp.exp(dot_t(query[:, lanes], k)).astype(BF)
            weights.append(p)
            tops.append(dot(p, v))
        return merge_windows(*tops, d), weights

    def finish(tops, weights, ones):
        top = jnp.concatenate(tops, axis=0)
        bottom = merge_windows(
            *[dot(jnp.concatenate([p[w] for p in weights], axis=0), ones[w]) for w in range(2)], d
        )
        return (top / bottom).astype(BF)

    def body(b, carry):
        start = pl.multiple_of(b * (block * tracks), block * tracks)
        settled = rows_ref[pl.ds(start, block * tracks), :].astype(F32)
        settled_norm = normed(settled).astype(BF)
        crossed = dot(settled_norm, ckv_ref[...])
        track_key = normed(crossed[:, :d]).astype(BF)
        track_value = crossed[:, d:].astype(BF)
        track_query = normed(dot(settled_norm, bq_ref[...]), tau).astype(BF)
        tops, weights = [], []
        for f in range(block):
            rows = slice(f * tracks, (f + 1) * tracks)
            pair, both = [], []
            for w, (first_lane, width, starts) in enumerate(wins):
                lanes = slice(first_lane, first_lane + width)
                p = jnp.exp(dot_t(stacked[w], track_key[rows, lanes])).astype(BF)
                p = jnp.concatenate([p[h * virt : (h + 1) * virt] for h in range(n_half)], axis=1)
                v = track_value[rows, lanes]
                v = jnp.concatenate([v * m for m in track_masks[w]], axis=0)
                both.append(p)
                pair.append(dot(p, v))
            tops.append(merge_windows(*pair, d))
            weights.append(both)
        cross_mixed = finish(tops, weights, track_ones)
        virtual = jnp.concatenate([init] * block, axis=0) + dot(cross_mixed, co_ref[...])
        selfed = dot(normed(virtual).astype(BF), sqkv_ref[...])
        query = normed(selfed[:, :d], tau).astype(BF)
        key = normed(selfed[:, d : 2 * d]).astype(BF)
        value = selfed[:, 2 * d :].astype(BF)
        tops, weights = [], []
        for f in range(block):
            rows = slice(f * virt, (f + 1) * virt)
            t, p = virtual_attention(query[rows], key[rows], value[rows])
            tops.append(t)
            weights.append(p)
        virtual = virtual + dot(finish(tops, weights, virt_ones), so_ref[...])
        backed = dot(normed(virtual).astype(BF), bkv_ref[...])
        key = normed(backed[:, :d]).astype(BF)
        value = backed[:, d:].astype(BF)
        tops, weights = [], []
        for f in range(block):
            rows = slice(f * virt, (f + 1) * virt)
            t, p = virtual_attention(track_query[f * tracks : (f + 1) * tracks], key[rows], value[rows])
            tops.append(t)
            weights.append(p)
        tracked = settled + dot(finish(tops, weights, virt_ones), bo_ref[...])
        rows_ref[pl.ds(start, block * tracks), :] = tracked.astype(BF)
        return carry

    lax.fori_loop(0, frames // block, body, 0)
    back = regroup(group, frames, True)
    for g in range(total // group):
        moved = jnp.concatenate(
            [rows_ref[f * tracks + g * part : f * tracks + (g + 1) * part, :] for f in range(frames)], axis=0
        )
        out_ref[g * group : (g + 1) * group, :] = dot(back, moved).astype(BF)


def virtual_part(x, frames, weights):
    block = min(frames, 4)
    group = max(256, 16 * frames)
    whole = pl.BlockSpec(memory_space=pltpu.VMEM)
    return pl.pallas_call(
        functools.partial(virtual_kernel, frames, block, group),
        out_shape=jax.ShapeDtypeStruct(x.shape, BF),
        in_specs=[whole] * (1 + len(weights)),
        out_specs=whole,
        scratch_shapes=[pltpu.VMEM(x.shape, BF)],
        compiler_params=pltpu.CompilerParams(vmem_limit_bytes=48 * 1024 * 1024),
        name="virtual_part",
    )(x, *weights)


def per_device(spots, tokens, first_frame, visible, *weights):
    time_weights, virtual_weights = weights[:4], weights[4:]
    tracks, half, d = tokens.shape
    mine = tracks // 2
    rows = half // spots
    core = lax.axis_index("frames")
    own = lax.dynamic_slice_in_dim(tokens, core * mine, mine, 0)
    away = lax.dynamic_slice_in_dim(tokens, (1 - core) * mine, mine, 0)
    other = lax.ppermute(away, "frames", [(0, 1), (1, 0)])
    where = jnp.stack([core, core * mine]).astype(jnp.int32)
    settled = time_part(own, other, first_frame, visible, where, time_weights, spots, 2)
    settled = settled.reshape(spots * 2, mine, rows, d)
    spread = lax.all_to_all(settled, ("tracks", "frames"), split_axis=0, concat_axis=0, tiled=True)
    tracked = virtual_part(spread.reshape(-1, d), rows, virtual_weights)
    tracked = tracked.reshape(spots, tracks, rows, d)
    joined = lax.all_to_all(tracked, "tracks", split_axis=0, concat_axis=0, tiled=True)
    return jnp.transpose(joined, (1, 0, 2, 3)).reshape(tracks, half, d)


def solution(mesh):
    spots = mesh.shape["tracks"]
    placed = (
        P(("groups", "tracks"), "frames", None),
        P(("groups", "tracks")),
        P(("groups", "tracks"), None),
    ) + (P(),) * 13
    return jax.shard_map(
        functools.partial(per_device, spots),
        mesh=mesh,
        in_specs=placed,
        out_specs=P(("groups", "tracks"), "frames", None),
        check_vma=False,
    )
```

```python
import functools

import jax
import jax.numpy as jnp
from jax import lax
from jax.experimental import pallas as pl
from jax.experimental.pallas import tpu as pltpu
from jax.sharding import PartitionSpec as P

HEADS = 8
HALF = HEADS // 2
EPS = 1e-06
BF = jnp.bfloat16
F32 = jnp.float32
VMEM = 62 * 1024 * 1024


def dot(a, b):
    return lax.dot_general(a, b, (((1,), (0,)), ((), ())), preferred_element_type=F32)


def dot_t(a, b):
    return lax.dot_general(a, b, (((1,), (1,)), ((), ())), preferred_element_type=F32)


def normed(x, scale=None):
    r = lax.rsqrt(jnp.mean(x * x, axis=-1, keepdims=True) + EPS)
    return x * (r if scale is None else r * scale)


def gelu(x):
    c = 0.7978845608028654
    h = 0.5 * x
    return h + h * jnp.tanh(x * (c + (c * 0.044715) * (x * x)))


def iota(rows, columns, axis):
    return lax.broadcasted_iota(jnp.int32, (rows, columns), axis)


def within(lane, start, count):
    return (lane >= start) & (lane < start + count)


class Lanes:
    def __init__(self, d):
        self.d = d
        self.head = d // HEADS
        self.width = -(-HALF * self.head // 128) * 128
        self.over = 2 * self.width - d
        self.spare = self.width - HALF * self.head
        assert self.spare >= 16 * HALF and self.over == 128 and self.spare <= 64
        self.begin = (0, d - self.width)
        self.first = (0, self.spare)
        self.sums = (HALF * self.head, 0)

    def cut(self, x, w):
        return x[:, self.begin[w] : self.begin[w] + self.width]

    def heads(self, rows, w):
        lane = iota(rows, self.width, 1)
        return [jnp.where(within(lane, self.first[w] + h * self.head, self.head), 1.0, 0.0).astype(BF) for h in range(HALF)]

    def sum_lanes(self, rows, w):
        lane = iota(rows, self.width, 1)
        return [jnp.where(within(lane, self.sums[w] + 16 * h, 16), 1.0, 0.0).astype(BF) for h in range(HALF)]

    def with_ones(self, v, w):
        lane = iota(v.shape[0], self.width, 1)
        return jnp.where(within(lane, self.first[w], HALF * self.head), self.cut(v, w), 1.0)

    def choose(self, o, rows, w):
        lane = iota(rows, self.width, 1)
        out = o[:rows]
        for h in range(1, HALF):
            own = within(lane, self.first[w] + h * self.head, self.head) | within(lane, self.sums[w] + 16 * h, 16)
            out = jnp.where(own, o[h * rows : (h + 1) * rows], out)
        return out

    def divide(self, low, high):
        rows = low.shape[0]
        lane = iota(rows, 128, 1)
        cut = self.width - self.over
        low_part, high_part = low[:, cut:], high[:, : self.over]
        split = self.over - self.spare
        sums = 1.0 / jnp.where(lane < split, high_part, low_part)
        pieces = [low[:, i : i + 128] for i in range(0, cut, 128)]
        pieces.append(jnp.where(lane < split, low_part, high_part))
        pieces += [high[:, i : i + 128] for i in range(self.over, self.width, 128)]
        out = []
        for i, piece in enumerate(pieces):
            head = (lane + 128 * i) // self.head
            spot = jnp.where(head < HALF, self.sums[0] - cut + 16 * head, self.sums[1] + 16 * (head - HALF))
            out.append(piece * jnp.take_along_axis(sums, spot, axis=1))
        return jnp.concatenate(out, axis=1).astype(BF)


def settle(own, other, usable, qkv_ref, out_w_ref, expand_ref, shrink_ref):
    tracks = len(usable)
    d = own.shape[1]
    half = own.shape[0] // tracks
    lanes = Lanes(d)
    own_norm = normed(own).astype(BF)
    query = normed(dot(own_norm, qkv_ref[:, :d]), lanes.head**-0.5).astype(BF)
    both = dot(jnp.concatenate([own_norm, normed(other).astype(BF)], axis=0), qkv_ref[:, d:])
    key = normed(both[:, :d]).astype(BF)
    value = both[:, d:]
    masks = [lanes.heads(half, w) for w in range(2)]
    mixed = []
    for i in range(tracks):
        mine = slice(i * half, (i + 1) * half)
        away = slice((tracks + i) * half, (tracks + i + 1) * half)
        k = jnp.concatenate([key[mine], key[away]], axis=0)
        v = jnp.concatenate([value[mine], value[away]], axis=0)
        pair = []
        for w in range(2):
            q = lanes.cut(query[mine], w)
            scores = dot_t(jnp.concatenate([q * m for m in masks[w]], axis=0), lanes.cut(k, w))
            weights = jnp.exp(scores).astype(BF)
            use = jnp.concatenate([usable[i]] * (lanes.width // 128), axis=1)
            o = dot(weights, (lanes.with_ones(v, w) * use).astype(BF))
            pair.append(lanes.choose(o, half, w))
        mixed.append(lanes.divide(*pair))
    middle = own + dot(jnp.concatenate(mixed, axis=0), out_w_ref[...])
    hidden = gelu(dot(normed(middle).astype(BF), expand_ref[...])).astype(BF)
    return (middle + dot(hidden, shrink_ref[...])).astype(BF)


def usable_columns(core, first, seen):
    length = seen.shape[1]
    frame = iota(1, length, 1)
    use = (frame >= first) & ((seen == 1) | (frame == first))
    use = jnp.where(use, 1.0, 0.0)
    low, high = use[:, : length // 2], use[:, length // 2 :]
    use = jnp.concatenate([jnp.where(core == 0, low, high), jnp.where(core == 0, high, low)], axis=1)
    return jnp.transpose(jnp.broadcast_to(use, (128, length)), (1, 0))


def time_kernel(tps, begin, info_ref, first_ref, visible_ref, own_ref, other_ref, *refs):
    weights, outs, kept_ref = refs[:4], refs[4:-1], refs[-1]
    half, d = own_ref.shape[1:]
    step = pl.program_id(0)
    usable = []
    for i in range(tps):
        track = begin + step * tps + i
        usable.append(usable_columns(info_ref[0], first_ref[track], visible_ref[pl.ds(track, 1), :]))
    own = own_ref[...].reshape(tps * half, d).astype(F32)
    other = other_ref[...].reshape(tps * half, d).astype(F32)
    settled = settle(own, other, usable, *weights)
    if len(outs[0].shape) == 3 and len(outs) == 1 and outs[0].shape[1] == half:
        outs[0][...] = settled.reshape(tps, half, d)
        return
    pieces = len(outs) > 1
    spots = len(outs) if pieces else outs[0].shape[0]
    rows = half // spots
    if not pieces:
        for t in range(spots):
            for i in range(tps):
                at = i * half + t * rows
                outs[0][t, i * rows : (i + 1) * rows, :] = settled[at : at + rows]
        return
    kept_ref[...] = settled
    for k in range(spots):
        t = lax.rem(info_ref[1] + k, spots)
        for i in range(tps):
            at = pl.multiple_of(i * half + t * rows, rows)
            outs[k][i * rows : (i + 1) * rows, :] = kept_ref[pl.ds(at, rows), :]


def full(shape):
    return pl.BlockSpec(shape, lambda *_: (0,) * len(shape))


def time_part(tokens, other, first_frame, visible, info, weights, spots, form, begin, count, after):
    _, half, d = tokens.shape
    rows = half // spots
    tps = 2
    if form == "tracks":
        shapes, blocks = [(count, half, d)], [pl.BlockSpec((tps, half, d), lambda i, *_: (i, 0, 0))]
    elif form == "dense":
        shapes, blocks = [(spots, count * rows, d)], [pl.BlockSpec((spots, tps * rows, d), lambda i, *_: (0, i, 0))]
    else:
        shapes, blocks = [(count * rows, d)] * spots, [pl.BlockSpec((tps * rows, d), lambda i, *_: (i, 0))] * spots
    total = count * half
    block = pl.BlockSpec((tps, half, d), lambda i, *_: (i, 0, 0))
    kernel = functools.partial(time_kernel, tps, begin)
    extra = [] if after is None else [after]
    if extra:
        inner = kernel

        def kernel(info_ref, first_ref, after_ref, *refs):
            inner(info_ref, first_ref, *refs)

    return pl.pallas_call(
        kernel,
        out_shape=[jax.ShapeDtypeStruct(s, BF) for s in shapes],
        grid_spec=pltpu.PrefetchScalarGridSpec(
            num_scalar_prefetch=2,
            grid=(count // tps,),
            in_specs=[pl.BlockSpec(memory_space=pl.ANY)] * len(extra)
            + [full(visible.shape), pl.BlockSpec((tps, half, d), lambda i, *_: (begin // tps + i, 0, 0)), block]
            + [full(w.shape) for w in weights],
            out_specs=blocks,
            scratch_shapes=[pltpu.VMEM((tps * half, d), BF)],
        ),
        compiler_params=pltpu.CompilerParams(vmem_limit_bytes=VMEM),
        cost_estimate=pl.CostEstimate(flops=total * 5_000_000, bytes_accessed=total * d * 4, transcendentals=total * 3600),
        name="time_part",
    )(info, first_frame, *extra, visible, tokens, other, *weights)


def gather_matrix(out_rows, in_rows, source):
    r, c = iota(out_rows, in_rows, 0), iota(out_rows, in_rows, 1)
    return jnp.where(c == source(r), 1.0, 0.0).astype(BF)


class Server:
    def __init__(self, weights):
        init_ref, cq_ref, self.ckv, self.co, self.sqkv, self.so, self.bq, self.bkv, self.bo = weights
        self.init = init_ref[...].astype(F32)
        self.virt, self.d = self.init.shape
        self.lanes = lanes = Lanes(self.d)
        self.tau = lanes.head**-0.5
        vq = normed(dot(normed(self.init).astype(BF), cq_ref[...]), self.tau).astype(BF)
        self.masks = [lanes.heads(self.virt, w) for w in range(2)]
        self.sums = [lanes.sum_lanes(self.virt, w) for w in range(2)]
        self.stacked = [
            jnp.concatenate([lanes.cut(vq, w) * m for m in self.masks[w]], axis=0) for w in range(2)
        ]

    def attend(self, query, key, value):
        lanes, pair = self.lanes, []
        for w in range(2):
            k, v = lanes.cut(key, w), lanes.cut(value, w)
            ks = jnp.concatenate([k * m for m in self.masks[w]], axis=0)
            vs = jnp.concatenate([v * m + s for m, s in zip(self.masks[w], self.sums[w])], axis=0)
            pair.append(dot(jnp.exp(dot_t(lanes.cut(query, w), ks)).astype(BF), vs))
        return pair

    def divide(self, pairs):
        return self.lanes.divide(*[jnp.concatenate([p[w] for p in pairs], axis=0) for w in range(2)])

    def run(self, settled, frames):
        d, lanes, virt = self.d, self.lanes, self.virt
        tracks = settled.shape[0] // frames
        settled_norm = normed(settled).astype(BF)
        crossed = dot(settled_norm, self.ckv[...])
        track_key = normed(crossed[:, :d]).astype(BF)
        track_value = crossed[:, d:]
        track_query = normed(dot(settled_norm, self.bq[...]), self.tau).astype(BF)
        ones = [lanes.with_ones(track_value, w).astype(BF) for w in range(2)]
        pairs = []
        for f in range(frames):
            rows = slice(f * tracks, (f + 1) * tracks)
            pair = []
            for w in range(2):
                p = jnp.exp(dot_t(self.stacked[w], lanes.cut(track_key[rows], w))).astype(BF)
                pair.append(lanes.choose(dot(p, ones[w][rows]), virt, w))
            pairs.append(pair)
        virtual = jnp.concatenate([self.init] * frames, axis=0) + dot(self.divide(pairs), self.co[...])
        selfed = dot(normed(virtual).astype(BF), self.sqkv[...])
        query = normed(selfed[:, :d], self.tau).astype(BF)
        key = normed(selfed[:, d : 2 * d]).astype(BF)
        value = selfed[:, 2 * d :].astype(BF)
        at = [slice(f * virt, (f + 1) * virt) for f in range(frames)]
        mixed = self.divide([self.attend(query[r], key[r], value[r]) for r in at])
        virtual = virtual + dot(mixed, self.so[...])
        backed = dot(normed(virtual).astype(BF), self.bkv[...])
        key = normed(backed[:, :d]).astype(BF)
        value = backed[:, d:].astype(BF)
        mixed = self.divide(
            [self.attend(track_query[f * tracks : (f + 1) * tracks], key[r], value[r]) for f, r in enumerate(at)]
        )
        return (settled + dot(mixed, self.bo[...])).astype(BF)


def rows_kernel(frames, block, group, x_ref, *refs):
    weights, out_ref, rows_ref = refs[:-2], refs[-2], refs[-1]
    total = x_ref.shape[0]
    tracks = total // frames
    part = group // frames
    there = gather_matrix(group, group, lambda r: (r % part) * frames + r // part)
    for g in range(total // group):
        moved = dot(there, x_ref[g * group : (g + 1) * group, :]).astype(BF)
        for f in range(frames):
            rows_ref[f * tracks + g * part : f * tracks + (g + 1) * part, :] = moved[f * part : (f + 1) * part]
    server = Server(weights)

    def body(b, carry):
        at = pl.ds(pl.multiple_of(b * (block * tracks), block * tracks), block * tracks)
        rows_ref[at, :] = server.run(rows_ref[at, :].astype(F32), block)
        return carry

    lax.fori_loop(0, frames // block, body, 0)
    back = gather_matrix(group, group, lambda r: (r % frames) * part + r // frames)
    for g in range(total // group):
        moved = jnp.concatenate(
            [rows_ref[f * tracks + g * part : f * tracks + (g + 1) * part, :] for f in range(frames)], axis=0
        )
        out_ref[g * group : (g + 1) * group, :] = dot(back, moved).astype(BF)


def rows_part(x, frames, weights):
    return pl.pallas_call(
        functools.partial(rows_kernel, frames, min(frames, 4), max(256, 16 * frames)),
        out_shape=jax.ShapeDtypeStruct(x.shape, BF),
        grid=(1,),
        in_specs=[full(a.shape) for a in (x, *weights)],
        out_specs=full(x.shape),
        scratch_shapes=[pltpu.VMEM(x.shape, BF)],
        compiler_params=pltpu.CompilerParams(vmem_limit_bytes=VMEM),
        name="rows_part",
    )(x, *weights)


def frames_kernel(spots, begin, frames, block, pieces, info_ref, dense_ref, *refs):
    xs, weights = refs[:spots], refs[spots : spots + 9]
    outs, rows_ref = refs[spots + 9 : -1], refs[-1]
    depth = dense_ref.shape[1] + xs[0].shape[0]
    span = pieces
    both = depth // span
    tracks = spots * both
    pick = gather_matrix(frames * both, depth, lambda r: (r % both) * span + begin + r // both)
    for k in range(spots):
        rows = jnp.concatenate([dense_ref[lax.rem(info_ref[1] + spots - k, spots)], xs[k][...]], axis=0)
        moved = dot(pick, rows).astype(BF)
        for f in range(frames):
            rows_ref[f * tracks + k * both : f * tracks + (k + 1) * both, :] = moved[f * both : (f + 1) * both]
    server = Server(weights)

    def body(b, carry):
        at = pl.ds(pl.multiple_of(b * (block * tracks), block * tracks), block * tracks)
        tracked = server.run(rows_ref[at, :].astype(F32), block)
        for f in range(block):
            to = pl.ds(pl.multiple_of((b * block + f) * both, both), both)
            for k in range(spots):
                rows = tracked[f * tracks + k * both : f * tracks + (k + 1) * both]
                if len(outs) > 1:
                    outs[k][to, :] = rows
                else:
                    outs[0][lax.rem(info_ref[1] + spots - k, spots), to, :] = rows
        return carry

    lax.fori_loop(0, frames // block, body, 0)


def frames_part(dense, xs, info, span, form, begin, frames, block, weights):
    spots, _, d = dense.shape
    both = (dense.shape[1] + xs[0].shape[0]) // span
    if form == "dense":
        shapes = [(spots, frames * both, d)]
    else:
        shapes = [(frames * both, d)] * spots
    rows = frames * spots * both
    return pl.pallas_call(
        functools.partial(frames_kernel, spots, begin, frames, block, span),
        out_shape=[jax.ShapeDtypeStruct(s, BF) for s in shapes],
        grid_spec=pltpu.PrefetchScalarGridSpec(
            num_scalar_prefetch=1,
            grid=(1,),
            in_specs=[full(a.shape) for a in (dense, *xs, *weights)],
            out_specs=[full(s) for s in shapes],
            scratch_shapes=[pltpu.VMEM((rows, d), BF)],
        ),
        compiler_params=pltpu.CompilerParams(vmem_limit_bytes=VMEM),
        cost_estimate=pl.CostEstimate(flops=rows * 10_000_000, bytes_accessed=rows * d * 4, transcendentals=rows * 2000),
        name="frames_part",
    )(info, dense, *xs, *weights)


def home_kernel(spots, info_ref, dense_ref, *refs):
    xs, out_ref = refs[:-1], refs[-1]
    tracks, _, d = out_ref.shape
    depth = dense_ref.shape[1] + xs[0].shape[0]
    span = depth // tracks
    pick = gather_matrix(depth, depth, lambda r: (r % span) * tracks + r // span)
    for k in range(spots):
        t = lax.rem(info_ref[1] + k, spots)
        rows = jnp.concatenate([dense_ref[t], xs[k][...]], axis=0)
        at = pl.ds(pl.multiple_of(t * span, span), span)
        out_ref[:, at, :] = dot(pick, rows).astype(BF).reshape(tracks, span, d)


def home(dense, xs, info, tracks):
    spots, _, d = dense.shape
    out = (tracks, spots * (dense.shape[1] + xs[0].shape[0]) // tracks, d)
    return pl.pallas_call(
        functools.partial(home_kernel, spots),
        out_shape=jax.ShapeDtypeStruct(out, BF),
        grid_spec=pltpu.PrefetchScalarGridSpec(
            num_scalar_prefetch=1,
            grid=(1,),
            in_specs=[full(a.shape) for a in (dense, *xs)],
            out_specs=full(out),
        ),
        compiler_params=pltpu.CompilerParams(vmem_limit_bytes=VMEM),
        name="home",
    )(info, dense, *xs)


def exchange(x):
    return lax.all_to_all(x, "tracks", split_axis=0, concat_axis=0, tiled=True)


def swap_cores(x):
    return lax.ppermute(x, "frames", [(0, 1), (1, 0)])


def shift(xs, spots, sign):
    return [xs[0]] + [
        lax.ppermute(xs[k], "tracks", [(i, (i + sign * k) % spots) for i in range(spots)]) for k in range(1, spots)
    ]


def simple(spots, tokens, first_frame, visible, info, time_weights, virtual_weights):
    tracks, half, d = tokens.shape
    rows = half // spots
    (settled,) = time_part(
        tokens, swap_cores(tokens), first_frame, visible, info, time_weights, spots, "tracks", 0, tracks, None
    )
    settled = jnp.transpose(settled.reshape(tracks, spots, rows, d), (1, 0, 2, 3))
    tracked = rows_part(exchange(settled).reshape(-1, d), rows, virtual_weights)
    joined = exchange(tracked.reshape(spots, tracks, rows, d))
    return jnp.transpose(joined, (1, 0, 2, 3)).reshape(tracks, half, d)


def pipelined(spots, tokens, first_frame, visible, info, time_weights, virtual_weights):
    tracks, half, d = tokens.shape
    rows = half // spots
    n = FIRST_TRACKS
    common = (first_frame, visible, info, time_weights, spots)
    (dense,) = time_part(tokens, swap_cores(tokens[:n]), *common, "dense", 0, n, None)
    pieces = time_part(tokens, swap_cores(tokens[n:]), *common, "pieces", n, tracks - n, dense)
    dense = exchange(dense)
    pieces = shift(pieces, spots, 1)
    m = FIRST_FRAMES
    (first,) = frames_part(dense, pieces, info, rows, "dense", 0, m, BLOCK, virtual_weights)
    rest = frames_part(dense, pieces, info, rows, "pieces", m, rows - m, BLOCK, virtual_weights)
    return home(exchange(first), shift(rest, spots, -1), info, tracks)


def per_device(spots, tokens, first_frame, visible, *weights):
    tracks, half, _ = tokens.shape
    rows = half // spots
    fits = tracks % 16 == 0 and rows % 16 == 0 and FIRST_TRACKS < tracks and FIRST_FRAMES < rows
    info = jnp.stack([lax.axis_index("frames"), lax.axis_index("tracks")]).astype(jnp.int32)
    run = pipelined if fits else simple
    return run(spots, tokens, first_frame, visible, info, weights[:4], weights[4:])


FIRST_TRACKS = 8
FIRST_FRAMES = 8
BLOCK = 4


def solution(mesh):
    rows = ("groups", "tracks")
    placed = (P(rows, "frames", None), P(rows), P(rows, None)) + (P(),) * 13
    return jax.shard_map(
        functools.partial(per_device, mesh.shape["tracks"]),
        mesh=mesh,
        in_specs=placed,
        out_specs=P(rows, "frames", None),
        check_vma=False,
    )
```

```python
import functools

import jax
import jax.numpy as jnp
from jax import lax
from jax.experimental import pallas as pl
from jax.experimental.pallas import tpu as pltpu
from jax.sharding import PartitionSpec as P

HEADS = 8
HALF = HEADS // 2
EPS = 1e-06
BF = jnp.bfloat16
F32 = jnp.float32
VMEM = 62 * 1024 * 1024


def dot(a, b):
    return lax.dot_general(a, b, (((1,), (0,)), ((), ())), preferred_element_type=F32)


def dot_t(a, b):
    return lax.dot_general(a, b, (((1,), (1,)), ((), ())), preferred_element_type=F32)


def normed(x, scale=None):
    r = lax.rsqrt(jnp.mean(x * x, axis=-1, keepdims=True) + EPS)
    return x * (r if scale is None else r * scale)


def gelu(x):
    c = 0.7978845608028654
    h = 0.5 * x
    return h + h * jnp.tanh(x * (c + (c * 0.044715) * (x * x)))


def iota(rows, columns, axis):
    return lax.broadcasted_iota(jnp.int32, (rows, columns), axis)


def within(lane, start, count):
    return (lane >= start) & (lane < start + count)


class Lanes:
    def __init__(self, d):
        self.d = d
        self.head = d // HEADS
        self.width = -(-HALF * self.head // 128) * 128
        self.over = 2 * self.width - d
        self.spare = self.width - HALF * self.head
        assert self.spare >= 16 * HALF and self.over == 128 and self.spare <= 64
        self.begin = (0, d - self.width)
        self.first = (0, self.spare)
        self.sums = (HALF * self.head, 0)

    def cut(self, x, w):
        return x[:, self.begin[w] : self.begin[w] + self.width]

    def heads(self, rows, w):
        lane = iota(rows, self.width, 1)
        return [jnp.where(within(lane, self.first[w] + h * self.head, self.head), 1.0, 0.0).astype(BF) for h in range(HALF)]

    def with_ones(self, v, w):
        lane = iota(v.shape[0], self.width, 1)
        return jnp.where(within(lane, self.first[w], HALF * self.head), self.cut(v, w), 1.0)

    def choose(self, o, rows, w):
        lane = iota(rows, self.width, 1)
        out = o[:rows]
        for h in range(1, HALF):
            own = within(lane, self.first[w] + h * self.head, self.head) | within(lane, self.sums[w] + 16 * h, 16)
            out = jnp.where(own, o[h * rows : (h + 1) * rows], out)
        return out

    def divide(self, low, high):
        rows = low.shape[0]
        lane = iota(rows, 128, 1)
        cut = self.width - self.over
        low_part, high_part = low[:, cut:], high[:, : self.over]
        split = self.over - self.spare
        sums = 1.0 / jnp.where(lane < split, high_part, low_part)
        pieces = [low[:, i : i + 128] for i in range(0, cut, 128)]
        pieces.append(jnp.where(lane < split, low_part, high_part))
        pieces += [high[:, i : i + 128] for i in range(self.over, self.width, 128)]
        out = []
        for i, piece in enumerate(pieces):
            head = (lane + 128 * i) // self.head
            spot = jnp.where(head < HALF, self.sums[0] - cut + 16 * head, self.sums[1] + 16 * (head - HALF))
            out.append(piece * jnp.take_along_axis(sums, spot, axis=1))
        return jnp.concatenate(out, axis=1).astype(BF)


def settle(own, other, usable, qkv_ref, out_w_ref, expand_ref, shrink_ref):
    tracks = len(usable)
    d = own.shape[1]
    half = own.shape[0] // tracks
    lanes = Lanes(d)
    own_norm = normed(own).astype(BF)
    query = normed(dot(own_norm, qkv_ref[:, :d]), lanes.head**-0.5).astype(BF)
    both = dot(jnp.concatenate([own_norm, normed(other).astype(BF)], axis=0), qkv_ref[:, d:])
    key = normed(both[:, :d]).astype(BF)
    value = both[:, d:]
    masks = [lanes.heads(half, w) for w in range(2)]
    mixed = []
    for i in range(tracks):
        mine = slice(i * half, (i + 1) * half)
        away = slice((tracks + i) * half, (tracks + i + 1) * half)
        k = jnp.concatenate([key[mine], key[away]], axis=0)
        v = jnp.concatenate([value[mine], value[away]], axis=0)
        pair = []
        for w in range(2):
            q = lanes.cut(query[mine], w)
            scores = dot_t(jnp.concatenate([q * m for m in masks[w]], axis=0), lanes.cut(k, w))
            weights = jnp.exp(scores).astype(BF)
            use = jnp.concatenate([usable[i]] * (lanes.width // 128), axis=1)
            o = dot(weights, (lanes.with_ones(v, w) * use).astype(BF))
            pair.append(lanes.choose(o, half, w))
        mixed.append(lanes.divide(*pair))
    middle = own + dot(jnp.concatenate(mixed, axis=0), out_w_ref[...])
    hidden = gelu(dot(normed(middle).astype(BF), expand_ref[...])).astype(BF)
    return middle + dot(hidden, shrink_ref[...])


def usable_columns(core, first, seen):
    length = seen.shape[1]
    frame = iota(1, length, 1)
    use = (frame >= first) & ((seen == 1) | (frame == first))
    use = jnp.where(use, 1.0, 0.0)
    low, high = use[:, : length // 2], use[:, length // 2 :]
    use = jnp.concatenate([jnp.where(core == 0, low, high), jnp.where(core == 0, high, low)], axis=1)
    return jnp.transpose(jnp.broadcast_to(use, (128, length)), (1, 0))


def time_kernel(tps, begin, form, info_ref, first_ref, visible_ref, own_ref, other_ref, *refs):
    weights, outs, kept_ref = refs[:4], refs[4:-1], refs[-1]
    half, d = own_ref.shape[1:]
    step = pl.program_id(0)
    usable = []
    for i in range(tps):
        track = begin + step * tps + i
        usable.append(usable_columns(info_ref[0], first_ref[track], visible_ref[pl.ds(track, 1), :]))
    own = own_ref[...].reshape(tps * half, d).astype(F32)
    other = other_ref[...].reshape(tps * half, d).astype(F32)
    settled = settle(own, other, usable, *weights)
    if form == "tracks":
        outs[0][...] = settled.astype(BF).reshape(tps, half, d)
        return
    spots = outs[0].shape[0]
    rows = half // spots
    last = outs[0].shape[1] // tps
    first = rows - last
    for t in range(spots):
        at = [i * half + t * rows + first for i in range(tps)]
        outs[0][t] = jnp.concatenate([settled[a : a + last] for a in at], axis=0).astype(BF)
    if form == "dense":
        return
    kept_ref[...] = settled
    for k in range(spots):
        t = lax.rem(info_ref[1] + k, spots)
        at = [pl.multiple_of(i * half + t * rows, 8) for i in range(tps)]
        outs[1 + k][...] = jnp.concatenate([kept_ref[pl.ds(a, first), :] for a in at], axis=0).astype(BF)


def full(shape):
    return pl.BlockSpec(shape, lambda *_: (0,) * len(shape))


def time_part(tokens, other, first_frame, visible, info, weights, spots, form, first, begin, count, after):
    _, half, d = tokens.shape
    rows = half // spots
    tps = 4
    if form == "tracks":
        shapes, blocks = [(count, half, d)], [pl.BlockSpec((tps, half, d), lambda i, *_: (i, 0, 0))]
    else:
        last = rows - first
        shapes = [(spots, count * last, d)]
        blocks = [pl.BlockSpec((spots, tps * last, d), lambda i, *_: (0, i, 0))]
    if form == "split":
        shapes += [(count * first, d)] * spots
        blocks += [pl.BlockSpec((tps * first, d), lambda i, *_: (i, 0))] * spots
    total = count * half
    block = pl.BlockSpec((tps, half, d), lambda i, *_: (i, 0, 0))
    kernel = functools.partial(time_kernel, tps, begin, form)
    extra = [] if after is None else [after]
    if extra:
        inner = kernel

        def kernel(info_ref, first_ref, after_ref, *refs):
            inner(info_ref, first_ref, *refs)

    return pl.pallas_call(
        kernel,
        out_shape=[jax.ShapeDtypeStruct(s, BF) for s in shapes],
        grid_spec=pltpu.PrefetchScalarGridSpec(
            num_scalar_prefetch=2,
            grid=(count // tps,),
            in_specs=[pl.BlockSpec(memory_space=pl.ANY)] * len(extra)
            + [full(visible.shape), pl.BlockSpec((tps, half, d), lambda i, *_: (begin // tps + i, 0, 0)), block]
            + [full(w.shape) for w in weights],
            out_specs=blocks,
            scratch_shapes=[pltpu.VMEM((tps * half, d), F32)],
        ),
        compiler_params=pltpu.CompilerParams(vmem_limit_bytes=VMEM),
        cost_estimate=pl.CostEstimate(flops=total * 5_000_000, bytes_accessed=total * d * 4, transcendentals=total * 3600),
        name="time_part",
    )(info, first_frame, *extra, visible, tokens, other, *weights)


def gather_matrix(out_rows, in_rows, source):
    r, c = iota(out_rows, in_rows, 0), iota(out_rows, in_rows, 1)
    return jnp.where(c == source(r), 1.0, 0.0).astype(BF)


class Server:
    def __init__(self, weights):
        init_ref, cq_ref, self.ckv, self.co, self.sqkv, self.so, self.bq, self.bkv, self.bo = weights
        self.init = init_ref[...].astype(F32)
        self.virt, self.d = self.init.shape
        self.lanes = lanes = Lanes(self.d)
        self.tau = lanes.head**-0.5
        vq = normed(dot(normed(self.init).astype(BF), cq_ref[...]), self.tau).astype(BF)
        self.masks = [lanes.heads(self.virt, w) for w in range(2)]
        self.stacked = [
            jnp.concatenate([lanes.cut(vq, w) * m for m in self.masks[w]], axis=0) for w in range(2)
        ]

    def attend(self, query, key, value, masks):
        lanes, pair = self.lanes, []
        for w in range(2):
            q = lanes.cut(query, w)
            q = jnp.concatenate([q * m for m in masks[w]], axis=0)
            p = jnp.exp(dot_t(q, lanes.cut(key, w))).astype(BF)
            pair.append(lanes.choose(dot(p, value[w]), query.shape[0], w))
        return pair

    def divide(self, pairs):
        return self.lanes.divide(*[jnp.concatenate([p[w] for p in pairs], axis=0) for w in range(2)])

    def run(self, settled, frames):
        d, lanes, virt = self.d, self.lanes, self.virt
        tracks = settled.shape[0] // frames
        settled_norm = normed(settled).astype(BF)
        crossed = dot(settled_norm, self.ckv[...])
        track_key = normed(crossed[:, :d]).astype(BF)
        track_value = crossed[:, d:]
        track_query = normed(dot(settled_norm, self.bq[...]), self.tau).astype(BF)
        ones = [lanes.with_ones(track_value, w).astype(BF) for w in range(2)]
        pairs = []
        for f in range(frames):
            rows = slice(f * tracks, (f + 1) * tracks)
            pair = []
            for w in range(2):
                p = jnp.exp(dot_t(self.stacked[w], lanes.cut(track_key[rows], w))).astype(BF)
                pair.append(lanes.choose(dot(p, ones[w][rows]), virt, w))
            pairs.append(pair)
        virtual = jnp.concatenate([self.init] * frames, axis=0) + dot(self.divide(pairs), self.co[...])
        selfed = dot(normed(virtual).astype(BF), self.sqkv[...])
        query = normed(selfed[:, :d], self.tau).astype(BF)
        key = normed(selfed[:, d : 2 * d]).astype(BF)
        value = [lanes.with_ones(selfed[:, 2 * d :], w).astype(BF) for w in range(2)]
        at = [slice(f * virt, (f + 1) * virt) for f in range(frames)]
        mixed = self.divide([self.attend(query[r], key[r], [v[r] for v in value], self.masks) for r in at])
        virtual = virtual + dot(mixed, self.so[...])
        backed = dot(normed(virtual).astype(BF), self.bkv[...])
        key = normed(backed[:, :d]).astype(BF)
        value = [lanes.with_ones(backed[:, d:], w).astype(BF) for w in range(2)]
        masks = [lanes.heads(tracks, w) for w in range(2)]
        mixed = self.divide(
            [
                self.attend(track_query[f * tracks : (f + 1) * tracks], key[r], [v[r] for v in value], masks)
                for f, r in enumerate(at)
            ]
        )
        return (settled + dot(mixed, self.bo[...])).astype(BF)


def rows_kernel(frames, block, group, x_ref, *refs):
    weights, out_ref, rows_ref = refs[:-2], refs[-2], refs[-1]
    total = x_ref.shape[0]
    tracks = total // frames
    part = group // frames
    there = gather_matrix(group, group, lambda r: (r % part) * frames + r // part)
    for g in range(total // group):
        moved = dot(there, x_ref[g * group : (g + 1) * group, :]).astype(BF)
        for f in range(frames):
            rows_ref[f * tracks + g * part : f * tracks + (g + 1) * part, :] = moved[f * part : (f + 1) * part]
    server = Server(weights)

    def body(b, carry):
        at = pl.ds(pl.multiple_of(b * (block * tracks), block * tracks), block * tracks)
        rows_ref[at, :] = server.run(rows_ref[at, :].astype(F32), block)
        return carry

    lax.fori_loop(0, frames // block, body, 0)
    back = gather_matrix(group, group, lambda r: (r % frames) * part + r // frames)
    for g in range(total // group):
        moved = jnp.concatenate(
            [rows_ref[f * tracks + g * part : f * tracks + (g + 1) * part, :] for f in range(frames)], axis=0
        )
        out_ref[g * group : (g + 1) * group, :] = dot(back, moved).astype(BF)


def rows_part(x, frames, weights):
    return pl.pallas_call(
        functools.partial(rows_kernel, frames, min(frames, 4), max(256, 16 * frames)),
        out_shape=jax.ShapeDtypeStruct(x.shape, BF),
        grid=(1,),
        in_specs=[full(a.shape) for a in (x, *weights)],
        out_specs=full(x.shape),
        scratch_shapes=[pltpu.VMEM(x.shape, BF)],
        compiler_params=pltpu.CompilerParams(vmem_limit_bytes=VMEM),
        name="rows_part",
    )(x, *weights)


def frames_kernel(spots, n_out, spans, begins, frames, block, info_ref, dense_ref, *refs):
    n = len(refs) - 10 - n_out
    xs, weights, outs, rows_ref = refs[:n], refs[n : n + 9], refs[n + 9 : -1], refs[-1]
    counts = (dense_ref.shape[1] // spans[0], xs[0].shape[-2] // spans[1])
    both = sum(counts)
    tracks = spots * both
    depth = counts[0] * spans[0] + counts[1] * spans[1]

    def source(r):
        f, track = r // both, r % both
        rest = counts[0] * spans[0] + (track - counts[0]) * spans[1] + begins[1] + f
        return jnp.where(track < counts[0], track * spans[0] + begins[0] + f, rest)

    pick = gather_matrix(frames * both, depth, source)
    for k in range(spots):
        back = lax.rem(info_ref[1] + spots - k, spots)
        rows = jnp.concatenate([dense_ref[back], xs[k][...] if n > 1 else xs[0][back]], axis=0)
        moved = dot(pick, rows).astype(BF)
        for f in range(frames):
            rows_ref[f * tracks + k * both : f * tracks + (k + 1) * both, :] = moved[f * both : (f + 1) * both]
    server = Server(weights)
    for b in range(0, frames, block):
        tracked = server.run(rows_ref[b * tracks : (b + block) * tracks, :].astype(F32), block)
        for f in range(block):
            to = slice((b + f) * both, (b + f + 1) * both)
            for k in range(spots):
                rows = tracked[f * tracks + k * both : f * tracks + (k + 1) * both]
                if len(outs) > 1:
                    outs[k][to, :] = rows
                else:
                    outs[0][lax.rem(info_ref[1] + spots - k, spots), to, :] = rows


def frames_part(dense, xs, info, spans, begins, form, frames, block, weights):
    spots, _, d = dense.shape
    both = dense.shape[1] // spans[0] + xs[0].shape[-2] // spans[1]
    if form == "dense":
        shapes = [(spots, frames * both, d)]
    else:
        shapes = [(frames * both, d)] * spots
    rows = frames * spots * both
    return pl.pallas_call(
        functools.partial(frames_kernel, spots, len(shapes), spans, begins, frames, block),
        out_shape=[jax.ShapeDtypeStruct(s, BF) for s in shapes],
        grid_spec=pltpu.PrefetchScalarGridSpec(
            num_scalar_prefetch=1,
            grid=(1,),
            in_specs=[full(a.shape) for a in (dense, *xs, *weights)],
            out_specs=[full(s) for s in shapes],
            scratch_shapes=[pltpu.VMEM((rows, d), BF)],
        ),
        compiler_params=pltpu.CompilerParams(vmem_limit_bytes=VMEM),
        cost_estimate=pl.CostEstimate(flops=rows * 10_000_000, bytes_accessed=rows * d * 4, transcendentals=rows * 2000),
        name="frames_part",
    )(info, dense, *xs, *weights)


def home_kernel(spots, info_ref, dense_ref, *refs):
    xs, out_ref = refs[:-1], refs[-1]
    tracks, _, d = out_ref.shape
    depth = dense_ref.shape[1] + xs[0].shape[0]
    span = depth // tracks
    pick = gather_matrix(depth, depth, lambda r: (r % span) * tracks + r // span)
    for k in range(spots):
        t = lax.rem(info_ref[1] + k, spots)
        rows = jnp.concatenate([dense_ref[t], xs[k][...]], axis=0)
        at = pl.ds(pl.multiple_of(t * span, span), span)
        out_ref[:, at, :] = dot(pick, rows).astype(BF).reshape(tracks, span, d)


def home(dense, xs, info, tracks):
    spots, _, d = dense.shape
    out = (tracks, spots * (dense.shape[1] + xs[0].shape[0]) // tracks, d)
    return pl.pallas_call(
        functools.partial(home_kernel, spots),
        out_shape=jax.ShapeDtypeStruct(out, BF),
        grid_spec=pltpu.PrefetchScalarGridSpec(
            num_scalar_prefetch=1,
            grid=(1,),
            in_specs=[full(a.shape) for a in (dense, *xs)],
            out_specs=full(out),
        ),
        compiler_params=pltpu.CompilerParams(vmem_limit_bytes=VMEM // 2),
        name="home",
    )(info, dense, *xs)


def exchange(x):
    return lax.all_to_all(x, "tracks", split_axis=0, concat_axis=0, tiled=True)


def swap_cores(x):
    return lax.ppermute(x, "frames", [(0, 1), (1, 0)])


def shift(xs, spots, sign):
    return [xs[0]] + [
        lax.ppermute(xs[k], "tracks", [(i, (i + sign * k) % spots) for i in range(spots)]) for k in range(1, spots)
    ]


def simple(spots, tokens, first_frame, visible, info, time_weights, virtual_weights):
    tracks, half, d = tokens.shape
    rows = half // spots
    (settled,) = time_part(
        tokens, swap_cores(tokens), first_frame, visible, info, time_weights, spots, "tracks", 0, 0, tracks, None
    )
    settled = jnp.transpose(settled.reshape(tracks, spots, rows, d), (1, 0, 2, 3))
    tracked = rows_part(exchange(settled).reshape(-1, d), rows, virtual_weights)
    joined = exchange(tracked.reshape(spots, tracks, rows, d))
    return jnp.transpose(joined, (1, 0, 2, 3)).reshape(tracks, half, d)


def pipelined(spots, tokens, first_frame, visible, info, time_weights, virtual_weights):
    tracks, half, d = tokens.shape
    rows = half // spots
    n, m = FIRST_TRACKS, FIRST_FRAMES
    common = (first_frame, visible, info, time_weights, spots)
    (dense,) = time_part(tokens, swap_cores(tokens[:n]), *common, "dense", 0, 0, n, None)
    rest, *first = time_part(tokens, swap_cores(tokens[n:]), *common, "split", m, n, tracks - n, dense)
    dense, first, rest = exchange(dense), shift(first, spots, 1), exchange(rest)
    (first,) = frames_part(dense, first, info, (rows, m), (0, 0), "dense", m, BLOCK, virtual_weights)
    rest = frames_part(dense, [rest], info, (rows, rows - m), (m, 0), "pieces", rows - m, BLOCK, virtual_weights)
    return home(exchange(first), shift(rest, spots, -1), info, tracks)


def per_device(spots, tokens, first_frame, visible, *weights):
    tracks, half, _ = tokens.shape
    rows = half // spots
    fits = tracks % 16 == 0 and rows % 16 == 0 and (rows - FIRST_FRAMES) % 8 == 0 and FIRST_TRACKS < tracks and FIRST_FRAMES < rows
    info = jnp.stack([lax.axis_index("frames"), lax.axis_index("tracks")]).astype(jnp.int32)
    run = pipelined if fits else simple
    return run(spots, tokens, first_frame, visible, info, weights[:4], weights[4:])


FIRST_TRACKS = 8
FIRST_FRAMES = 8
BLOCK = 8


def solution(mesh):
    rows = ("groups", "tracks")
    placed = (P(rows, "frames", None), P(rows), P(rows, None)) + (P(),) * 13
    return jax.shard_map(
        functools.partial(per_device, mesh.shape["tracks"]),
        mesh=mesh,
        in_specs=placed,
        out_specs=P(rows, "frames", None),
        check_vma=False,
    )
```

```python
import functools

import jax
import jax.numpy as jnp
from jax import lax
from jax.experimental import pallas as pl
from jax.experimental.pallas import tpu as pltpu
from jax.sharding import PartitionSpec as P

HEADS = 8
HALF = HEADS // 2
EPS = 1e-06
BF = jnp.bfloat16
F32 = jnp.float32
VMEM = 62 * 1024 * 1024


def dot(a, b):
    return lax.dot_general(a, b, (((1,), (0,)), ((), ())), preferred_element_type=F32)


def dot_t(a, b):
    return lax.dot_general(a, b, (((1,), (1,)), ((), ())), preferred_element_type=F32)


def normed(x, scale=None):
    r = lax.rsqrt(jnp.mean(x * x, axis=-1, keepdims=True) + EPS)
    return x * (r if scale is None else r * scale)


def gelu(x):
    c = 0.7978845608028654
    h = 0.5 * x
    return h + h * jnp.tanh(x * (c + (c * 0.044715) * (x * x)))


def iota(rows, columns, axis):
    return lax.broadcasted_iota(jnp.int32, (rows, columns), axis)


def within(lane, start, count):
    return (lane >= start) & (lane < start + count)


class Lanes:
    def __init__(self, d):
        self.d = d
        self.head = d // HEADS
        self.width = -(-HALF * self.head // 128) * 128
        self.over = 2 * self.width - d
        self.spare = self.width - HALF * self.head
        assert self.spare >= 16 * HALF and self.over == 128 and self.spare <= 64
        self.begin = (0, d - self.width)
        self.first = (0, self.spare)
        self.sums = (HALF * self.head, 0)

    def cut(self, x, w):
        return x[:, self.begin[w] : self.begin[w] + self.width]

    def heads(self, rows, w):
        lane = iota(rows, self.width, 1)
        return [jnp.where(within(lane, self.first[w] + h * self.head, self.head), 1.0, 0.0).astype(BF) for h in range(HALF)]

    def with_ones(self, v, w):
        lane = iota(v.shape[0], self.width, 1)
        return jnp.where(within(lane, self.first[w], HALF * self.head), self.cut(v, w), 1.0)

    def choose(self, o, rows, w):
        lane = iota(rows, self.width, 1)
        out = o[:rows]
        for h in range(1, HALF):
            own = within(lane, self.first[w] + h * self.head, self.head) | within(lane, self.sums[w] + 16 * h, 16)
            out = jnp.where(own, o[h * rows : (h + 1) * rows], out)
        return out

    def divide(self, low, high):
        rows = low.shape[0]
        lane = iota(rows, 128, 1)
        cut = self.width - self.over
        low_part, high_part = low[:, cut:], high[:, : self.over]
        split = self.over - self.spare
        sums = 1.0 / jnp.where(lane < split, high_part, low_part)
        pieces = [low[:, i : i + 128] for i in range(0, cut, 128)]
        pieces.append(jnp.where(lane < split, low_part, high_part))
        pieces += [high[:, i : i + 128] for i in range(self.over, self.width, 128)]
        out = []
        for i, piece in enumerate(pieces):
            head = (lane + 128 * i) // self.head
            spot = jnp.where(head < HALF, self.sums[0] - cut + 16 * head, self.sums[1] + 16 * (head - HALF))
            out.append(piece * jnp.take_along_axis(sums, spot, axis=1))
        return jnp.concatenate(out, axis=1).astype(BF)


def settle(own, other, usable, qkv_ref, out_w_ref, expand_ref, shrink_ref):
    tracks = len(usable)
    d = own.shape[1]
    half = own.shape[0] // tracks
    lanes = Lanes(d)
    own_norm = normed(own).astype(BF)
    query = normed(dot(own_norm, qkv_ref[:, :d]), lanes.head**-0.5).astype(BF)
    both = dot(jnp.concatenate([own_norm, normed(other).astype(BF)], axis=0), qkv_ref[:, d:])
    key = normed(both[:, :d]).astype(BF)
    value = both[:, d:]
    masks = [lanes.heads(half, w) for w in range(2)]
    mixed = []
    def scored(i, w):
        mine = slice(i * half, (i + 1) * half)
        away = slice((tracks + i) * half, (tracks + i + 1) * half)
        k = jnp.concatenate([key[mine], key[away]], axis=0)
        q = lanes.cut(query[mine], w)
        return dot_t(jnp.concatenate([q * m for m in masks[w]], axis=0), lanes.cut(k, w))

    todo = [(i, w) for i in range(tracks) for w in range(2)]
    scores = [scored(*todo[0])]
    pair = []
    for at, (i, w) in enumerate(todo):
        if at + 1 < len(todo):
            scores.append(scored(*todo[at + 1]))
        mine = slice(i * half, (i + 1) * half)
        away = slice((tracks + i) * half, (tracks + i + 1) * half)
        v = jnp.concatenate([value[mine], value[away]], axis=0)
        weights = jnp.exp(scores[at]).astype(BF)
        use = jnp.concatenate([usable[i]] * (lanes.width // 128), axis=1)
        o = dot(weights, (lanes.with_ones(v, w) * use).astype(BF))
        pair.append(lanes.choose(o, half, w))
        if w == 1:
            mixed.append(lanes.divide(*pair))
            pair = []
    middle = own + dot(jnp.concatenate(mixed, axis=0), out_w_ref[...])
    hidden = gelu(dot(normed(middle).astype(BF), expand_ref[...])).astype(BF)
    return middle + dot(hidden, shrink_ref[...])


def usable_columns(core, first, seen):
    length = seen.shape[1]
    frame = iota(1, length, 1)
    use = (frame >= first) & ((seen == 1) | (frame == first))
    use = jnp.where(use, 1.0, 0.0)
    low, high = use[:, : length // 2], use[:, length // 2 :]
    use = jnp.concatenate([jnp.where(core == 0, low, high), jnp.where(core == 0, high, low)], axis=1)
    return jnp.transpose(jnp.broadcast_to(use, (128, length)), (1, 0))


def time_kernel(tps, begin, form, info_ref, first_ref, visible_ref, own_ref, other_ref, *refs):
    weights, outs, kept_ref = refs[:4], refs[4:-1], refs[-1]
    half, d = own_ref.shape[1:]
    step = pl.program_id(0)
    usable = []
    for i in range(tps):
        track = begin + step * tps + i
        usable.append(usable_columns(info_ref[0], first_ref[track], visible_ref[pl.ds(track, 1), :]))
    own = own_ref[...].reshape(tps * half, d).astype(F32)
    other = other_ref[...].reshape(tps * half, d).astype(F32)
    settled = settle(own, other, usable, *weights)
    if form == "tracks":
        outs[0][...] = settled.astype(BF).reshape(tps, half, d)
        return
    spots = outs[0].shape[0]
    rows = half // spots
    last = outs[0].shape[1] // tps
    first = rows - last
    for t in range(spots):
        at = [i * half + t * rows + first for i in range(tps)]
        outs[0][t] = jnp.concatenate([settled[a : a + last] for a in at], axis=0).astype(BF)
    if form == "dense":
        return
    kept_ref[...] = settled
    for k in range(spots):
        t = lax.rem(info_ref[1] + k, spots)
        at = [pl.multiple_of(i * half + t * rows, 8) for i in range(tps)]
        outs[1 + k][...] = jnp.concatenate([kept_ref[pl.ds(a, first), :] for a in at], axis=0).astype(BF)


def full(shape):
    return pl.BlockSpec(shape, lambda *_: (0,) * len(shape))


def time_part(tokens, other, first_frame, visible, info, weights, spots, form, first, begin, count, after):
    _, half, d = tokens.shape
    rows = half // spots
    tps = 4
    if form == "tracks":
        shapes, blocks = [(count, half, d)], [pl.BlockSpec((tps, half, d), lambda i, *_: (i, 0, 0))]
    else:
        last = rows - first
        shapes = [(spots, count * last, d)]
        blocks = [pl.BlockSpec((spots, tps * last, d), lambda i, *_: (0, i, 0))]
    if form == "split":
        shapes += [(count * first, d)] * spots
        blocks += [pl.BlockSpec((tps * first, d), lambda i, *_: (i, 0))] * spots
    total = count * half
    block = pl.BlockSpec((tps, half, d), lambda i, *_: (begin // tps + i, 0, 0))
    kernel = functools.partial(time_kernel, tps, begin, form)
    extra = [] if after is None else [after]
    if extra:
        inner = kernel

        def kernel(info_ref, first_ref, after_ref, *refs):
            inner(info_ref, first_ref, *refs)

    return pl.pallas_call(
        kernel,
        out_shape=[jax.ShapeDtypeStruct(s, BF) for s in shapes],
        grid_spec=pltpu.PrefetchScalarGridSpec(
            num_scalar_prefetch=2,
            grid=(count // tps,),
            in_specs=[pl.BlockSpec(memory_space=pl.ANY)] * len(extra)
            + [full(visible.shape), block, block]
            + [full(w.shape) for w in weights],
            out_specs=blocks,
            scratch_shapes=[pltpu.VMEM((tps * half, d), F32)],
        ),
        compiler_params=pltpu.CompilerParams(vmem_limit_bytes=VMEM),
        cost_estimate=pl.CostEstimate(flops=total * 5_000_000, bytes_accessed=total * d * 4, transcendentals=total * 3600),
        name="time_part",
    )(info, first_frame, *extra, visible, tokens, other, *weights)


def gather_matrix(out_rows, in_rows, source):
    r, c = iota(out_rows, in_rows, 0), iota(out_rows, in_rows, 1)
    return jnp.where(c == source(r), 1.0, 0.0).astype(BF)


class Server:
    def __init__(self, weights):
        init_ref, cq_ref, self.ckv, self.co, self.sqkv, self.so, self.bq, self.bkv, self.bo = weights
        self.init = init_ref[...].astype(F32)
        self.virt, self.d = self.init.shape
        self.lanes = lanes = Lanes(self.d)
        self.tau = lanes.head**-0.5
        vq = normed(dot(normed(self.init).astype(BF), cq_ref[...]), self.tau).astype(BF)
        self.masks = [lanes.heads(self.virt, w) for w in range(2)]
        self.stacked = [
            jnp.concatenate([lanes.cut(vq, w) * m for m in self.masks[w]], axis=0) for w in range(2)
        ]

    def attend(self, query, key, value, masks):
        lanes, pair = self.lanes, []
        for w in range(2):
            q = lanes.cut(query, w)
            q = jnp.concatenate([q * m for m in masks[w]], axis=0)
            p = jnp.exp(dot_t(q, lanes.cut(key, w))).astype(BF)
            pair.append(lanes.choose(dot(p, value[w]), query.shape[0], w))
        return pair

    def divide(self, pairs):
        return self.lanes.divide(*[jnp.concatenate([p[w] for p in pairs], axis=0) for w in range(2)])

    def run(self, settled, frames):
        d, lanes, virt = self.d, self.lanes, self.virt
        tracks = settled.shape[0] // frames
        settled_norm = normed(settled).astype(BF)
        crossed = dot(settled_norm, self.ckv[...])
        track_key = normed(crossed[:, :d]).astype(BF)
        track_value = crossed[:, d:]
        track_query = normed(dot(settled_norm, self.bq[...]), self.tau).astype(BF)
        ones = [lanes.with_ones(track_value, w).astype(BF) for w in range(2)]
        pairs = []
        for f in range(frames):
            rows = slice(f * tracks, (f + 1) * tracks)
            pair = []
            for w in range(2):
                p = jnp.exp(dot_t(self.stacked[w], lanes.cut(track_key[rows], w))).astype(BF)
                pair.append(lanes.choose(dot(p, ones[w][rows]), virt, w))
            pairs.append(pair)
        virtual = jnp.concatenate([self.init] * frames, axis=0) + dot(self.divide(pairs), self.co[...])
        selfed = dot(normed(virtual).astype(BF), self.sqkv[...])
        query = normed(selfed[:, :d], self.tau).astype(BF)
        key = normed(selfed[:, d : 2 * d]).astype(BF)
        value = [lanes.with_ones(selfed[:, 2 * d :], w).astype(BF) for w in range(2)]
        at = [slice(f * virt, (f + 1) * virt) for f in range(frames)]
        mixed = self.divide([self.attend(query[r], key[r], [v[r] for v in value], self.masks) for r in at])
        virtual = virtual + dot(mixed, self.so[...])
        backed = dot(normed(virtual).astype(BF), self.bkv[...])
        key = normed(backed[:, :d]).astype(BF)
        value = [lanes.with_ones(backed[:, d:], w).astype(BF) for w in range(2)]
        masks = [lanes.heads(tracks, w) for w in range(2)]
        mixed = self.divide(
            [
                self.attend(track_query[f * tracks : (f + 1) * tracks], key[r], [v[r] for v in value], masks)
                for f, r in enumerate(at)
            ]
        )
        return (settled + dot(mixed, self.bo[...])).astype(BF)


def rows_kernel(frames, block, group, x_ref, *refs):
    weights, out_ref, rows_ref = refs[:-2], refs[-2], refs[-1]
    total = x_ref.shape[0]
    tracks = total // frames
    part = group // frames
    there = gather_matrix(group, group, lambda r: (r % part) * frames + r // part)
    for g in range(total // group):
        moved = dot(there, x_ref[g * group : (g + 1) * group, :]).astype(BF)
        for f in range(frames):
            rows_ref[f * tracks + g * part : f * tracks + (g + 1) * part, :] = moved[f * part : (f + 1) * part]
    server = Server(weights)

    def body(b, carry):
        at = pl.ds(pl.multiple_of(b * (block * tracks), block * tracks), block * tracks)
        rows_ref[at, :] = server.run(rows_ref[at, :].astype(F32), block)
        return carry

    lax.fori_loop(0, frames // block, body, 0)
    back = gather_matrix(group, group, lambda r: (r % frames) * part + r // frames)
    for g in range(total // group):
        moved = jnp.concatenate(
            [rows_ref[f * tracks + g * part : f * tracks + (g + 1) * part, :] for f in range(frames)], axis=0
        )
        out_ref[g * group : (g + 1) * group, :] = dot(back, moved).astype(BF)


def rows_part(x, frames, weights):
    return pl.pallas_call(
        functools.partial(rows_kernel, frames, min(frames, 4), max(256, 16 * frames)),
        out_shape=jax.ShapeDtypeStruct(x.shape, BF),
        grid=(1,),
        in_specs=[full(a.shape) for a in (x, *weights)],
        out_specs=full(x.shape),
        scratch_shapes=[pltpu.VMEM(x.shape, BF)],
        compiler_params=pltpu.CompilerParams(vmem_limit_bytes=VMEM),
        name="rows_part",
    )(x, *weights)


def frames_kernel(spots, n_out, spans, begins, frames, block, info_ref, dense_ref, *refs):
    n = len(refs) - 10 - n_out
    xs, weights, outs, rows_ref = refs[:n], refs[n : n + 9], refs[n + 9 : -1], refs[-1]
    counts = (dense_ref.shape[1] // spans[0], xs[0].shape[-2] // spans[1])
    both = sum(counts)
    tracks = spots * both
    depth = counts[0] * spans[0] + counts[1] * spans[1]

    def source(r):
        f, track = r // both, r % both
        rest = counts[0] * spans[0] + (track - counts[0]) * spans[1] + begins[1] + f
        return jnp.where(track < counts[0], track * spans[0] + begins[0] + f, rest)

    pick = gather_matrix(frames * both, depth, source)
    for k in range(spots):
        back = lax.rem(info_ref[1] + spots - k, spots)
        rows = jnp.concatenate([dense_ref[back], xs[k][...] if n > 1 else xs[0][back]], axis=0)
        moved = dot(pick, rows).astype(BF)
        for f in range(frames):
            rows_ref[f * tracks + k * both : f * tracks + (k + 1) * both, :] = moved[f * both : (f + 1) * both]
    server = Server(weights)
    for b in range(0, frames, block):
        tracked = server.run(rows_ref[b * tracks : (b + block) * tracks, :].astype(F32), block)
        for f in range(block):
            to = slice((b + f) * both, (b + f + 1) * both)
            for k in range(spots):
                rows = tracked[f * tracks + k * both : f * tracks + (k + 1) * both]
                if len(outs) > 1:
                    outs[k][to, :] = rows
                else:
                    outs[0][lax.rem(info_ref[1] + spots - k, spots), to, :] = rows


def frames_part(dense, xs, info, spans, begins, form, frames, block, weights):
    spots, _, d = dense.shape
    both = dense.shape[1] // spans[0] + xs[0].shape[-2] // spans[1]
    if form == "dense":
        shapes = [(spots, frames * both, d)]
    else:
        shapes = [(frames * both, d)] * spots
    rows = frames * spots * both
    return pl.pallas_call(
        functools.partial(frames_kernel, spots, len(shapes), spans, begins, frames, block),
        out_shape=[jax.ShapeDtypeStruct(s, BF) for s in shapes],
        grid_spec=pltpu.PrefetchScalarGridSpec(
            num_scalar_prefetch=1,
            grid=(1,),
            in_specs=[full(a.shape) for a in (dense, *xs, *weights)],
            out_specs=[full(s) for s in shapes],
            scratch_shapes=[pltpu.VMEM((rows, d), BF)],
        ),
        compiler_params=pltpu.CompilerParams(vmem_limit_bytes=VMEM),
        cost_estimate=pl.CostEstimate(flops=rows * 10_000_000, bytes_accessed=rows * d * 4, transcendentals=rows * 2000),
        name="frames_part",
    )(info, dense, *xs, *weights)


def home_kernel(spots, info_ref, dense_ref, *refs):
    xs, out_ref = refs[:-1], refs[-1]
    tracks, _, d = out_ref.shape
    depth = dense_ref.shape[1] + xs[0].shape[0]
    span = depth // tracks
    pick = gather_matrix(depth, depth, lambda r: (r % span) * tracks + r // span)
    for k in range(spots):
        t = lax.rem(info_ref[1] + k, spots)
        rows = jnp.concatenate([dense_ref[t], xs[k][...]], axis=0)
        at = pl.ds(pl.multiple_of(t * span, span), span)
        out_ref[:, at, :] = dot(pick, rows).astype(BF).reshape(tracks, span, d)


def home(dense, xs, info, tracks):
    spots, _, d = dense.shape
    out = (tracks, spots * (dense.shape[1] + xs[0].shape[0]) // tracks, d)
    return pl.pallas_call(
        functools.partial(home_kernel, spots),
        out_shape=jax.ShapeDtypeStruct(out, BF),
        grid_spec=pltpu.PrefetchScalarGridSpec(
            num_scalar_prefetch=1,
            grid=(1,),
            in_specs=[full(a.shape) for a in (dense, *xs)],
            out_specs=full(out),
        ),
        compiler_params=pltpu.CompilerParams(vmem_limit_bytes=VMEM // 2),
        name="home",
    )(info, dense, *xs)


def exchange(x):
    return lax.all_to_all(x, "tracks", split_axis=0, concat_axis=0, tiled=True)


def swap_cores(x):
    return lax.ppermute(x, "frames", [(0, 1), (1, 0)])


def shift(xs, spots, sign):
    return [xs[0]] + [
        lax.ppermute(xs[k], "tracks", [(i, (i + sign * k) % spots) for i in range(spots)]) for k in range(1, spots)
    ]


def simple(spots, tokens, first_frame, visible, info, time_weights, virtual_weights):
    tracks, half, d = tokens.shape
    rows = half // spots
    (settled,) = time_part(
        tokens, swap_cores(tokens), first_frame, visible, info, time_weights, spots, "tracks", 0, 0, tracks, None
    )
    settled = jnp.transpose(settled.reshape(tracks, spots, rows, d), (1, 0, 2, 3))
    tracked = rows_part(exchange(settled).reshape(-1, d), rows, virtual_weights)
    joined = exchange(tracked.reshape(spots, tracks, rows, d))
    return jnp.transpose(joined, (1, 0, 2, 3)).reshape(tracks, half, d)


def pipelined(spots, tokens, first_frame, visible, info, time_weights, virtual_weights):
    tracks, half, d = tokens.shape
    rows = half // spots
    n, m = FIRST_TRACKS, FIRST_FRAMES
    common = (first_frame, visible, info, time_weights, spots)
    other = swap_cores(tokens)
    (dense,) = time_part(tokens, other, *common, "dense", 0, 0, n, None)
    rest, *first = time_part(tokens, other, *common, "split", m, n, tracks - n, dense)
    dense, first, rest = exchange(dense), shift(first, spots, 1), exchange(rest)
    (first,) = frames_part(dense, first, info, (rows, m), (0, 0), "dense", m, BLOCK, virtual_weights)
    rest = frames_part(dense, [rest], info, (rows, rows - m), (m, 0), "pieces", rows - m, BLOCK, virtual_weights)
    return home(exchange(first), shift(rest, spots, -1), info, tracks)


def per_device(spots, tokens, first_frame, visible, *weights):
    tracks, half, _ = tokens.shape
    rows = half // spots
    fits = tracks % 16 == 0 and rows % 16 == 0 and (rows - FIRST_FRAMES) % 8 == 0 and FIRST_TRACKS < tracks and FIRST_FRAMES < rows
    info = jnp.stack([lax.axis_index("frames"), lax.axis_index("tracks")]).astype(jnp.int32)
    run = pipelined if fits else simple
    return run(spots, tokens, first_frame, visible, info, weights[:4], weights[4:])


FIRST_TRACKS = 8
FIRST_FRAMES = 8
BLOCK = 8


def solution(mesh):
    rows = ("groups", "tracks")
    placed = (P(rows, "frames", None), P(rows), P(rows, None)) + (P(),) * 13
    return jax.shard_map(
        functools.partial(per_device, mesh.shape["tracks"]),
        mesh=mesh,
        in_specs=placed,
        out_specs=P(rows, "frames", None),
        check_vma=False,
    )
```

```python
import functools

import jax
import jax.numpy as jnp
from jax import lax
from jax.experimental import pallas as pl
from jax.experimental.pallas import tpu as pltpu
from jax.sharding import PartitionSpec as P

HEADS = 8
HALF = HEADS // 2
EPS = 1e-06
BF = jnp.bfloat16
F32 = jnp.float32
VMEM = 62 * 1024 * 1024


def dot(a, b):
    return lax.dot_general(a, b, (((1,), (0,)), ((), ())), preferred_element_type=F32)


def dot_t(a, b):
    return lax.dot_general(a, b, (((1,), (1,)), ((), ())), preferred_element_type=F32)


def normed(x, scale=None):
    r = lax.rsqrt(jnp.mean(x * x, axis=-1, keepdims=True) + EPS)
    return x * (r if scale is None else r * scale)


def gelu(x):
    c = 0.7978845608028654
    h = 0.5 * x
    return h + h * jnp.tanh(x * (c + (c * 0.044715) * (x * x)))


def iota(rows, columns, axis):
    return lax.broadcasted_iota(jnp.int32, (rows, columns), axis)


def within(lane, start, count):
    return (lane >= start) & (lane < start + count)


class Lanes:
    def __init__(self, d):
        self.d = d
        self.head = d // HEADS
        self.width = -(-HALF * self.head // 128) * 128
        self.over = 2 * self.width - d
        self.spare = self.width - HALF * self.head
        assert self.spare >= 16 * HALF and self.over == 128 and self.spare <= 64
        self.begin = (0, d - self.width)
        self.first = (0, self.spare)
        self.sums = (HALF * self.head, 0)

    def cut(self, x, w):
        return x[:, self.begin[w] : self.begin[w] + self.width]

    def heads(self, rows, w):
        lane = iota(rows, self.width, 1)
        return [jnp.where(within(lane, self.first[w] + h * self.head, self.head), 1.0, 0.0).astype(BF) for h in range(HALF)]

    def with_ones(self, v, w):
        lane = iota(v.shape[0], self.width, 1)
        return jnp.where(within(lane, self.first[w], HALF * self.head), self.cut(v, w), 1.0)

    def choose(self, o, rows, w):
        lane = iota(rows, self.width, 1)
        out = o[:rows]
        for h in range(1, HALF):
            own = within(lane, self.first[w] + h * self.head, self.head) | within(lane, self.sums[w] + 16 * h, 16)
            out = jnp.where(own, o[h * rows : (h + 1) * rows], out)
        return out

    def divide(self, low, high):
        rows = low.shape[0]
        lane = iota(rows, 128, 1)
        cut = self.width - self.over
        low_part, high_part = low[:, cut:], high[:, : self.over]
        split = self.over - self.spare
        sums = 1.0 / jnp.where(lane < split, high_part, low_part)
        pieces = [low[:, i : i + 128] for i in range(0, cut, 128)]
        pieces.append(jnp.where(lane < split, low_part, high_part))
        pieces += [high[:, i : i + 128] for i in range(self.over, self.width, 128)]
        out = []
        for i, piece in enumerate(pieces):
            head = (lane + 128 * i) // self.head
            spot = jnp.where(head < HALF, self.sums[0] - cut + 16 * head, self.sums[1] + 16 * (head - HALF))
            out.append(piece * jnp.take_along_axis(sums, spot, axis=1))
        return jnp.concatenate(out, axis=1).astype(BF)


def settle(own, other, usable, qkv_ref, out_w_ref, expand_ref, shrink_ref):
    tracks = len(usable)
    d = own.shape[1]
    half = own.shape[0] // tracks
    lanes = Lanes(d)
    own_norm = normed(own).astype(BF)
    query = normed(dot(own_norm, qkv_ref[:, :d]), lanes.head**-0.5).astype(BF)
    both = dot(jnp.concatenate([own_norm, normed(other).astype(BF)], axis=0), qkv_ref[:, d:])
    key = normed(both[:, :d]).astype(BF)
    value = both[:, d:]
    masks = [lanes.heads(half, w) for w in range(2)]
    mixed = []
    def scored(i, w):
        mine = slice(i * half, (i + 1) * half)
        away = slice((tracks + i) * half, (tracks + i + 1) * half)
        k = jnp.concatenate([key[mine], key[away]], axis=0)
        q = lanes.cut(query[mine], w)
        return dot_t(jnp.concatenate([q * m for m in masks[w]], axis=0), lanes.cut(k, w))

    todo = [(i, w) for i in range(tracks) for w in range(2)]
    scores = [scored(*todo[0])]
    pair = []
    for at, (i, w) in enumerate(todo):
        if at + 1 < len(todo):
            scores.append(scored(*todo[at + 1]))
        mine = slice(i * half, (i + 1) * half)
        away = slice((tracks + i) * half, (tracks + i + 1) * half)
        v = jnp.concatenate([value[mine], value[away]], axis=0)
        weights = jnp.exp(scores[at]).astype(BF)
        use = jnp.concatenate([usable[i]] * (lanes.width // 128), axis=1)
        o = dot(weights, (lanes.with_ones(v, w) * use).astype(BF))
        pair.append(lanes.choose(o, half, w))
        if w == 1:
            mixed.append(lanes.divide(*pair))
            pair = []
    middle = own + dot(jnp.concatenate(mixed, axis=0), out_w_ref[...])
    hidden = gelu(dot(normed(middle).astype(BF), expand_ref[...])).astype(BF)
    return middle + dot(hidden, shrink_ref[...])


def usable_columns(core, first, seen):
    length = seen.shape[1]
    frame = iota(1, length, 1)
    use = (frame >= first) & ((seen == 1) | (frame == first))
    use = jnp.where(use, 1.0, 0.0)
    low, high = use[:, : length // 2], use[:, length // 2 :]
    use = jnp.concatenate([jnp.where(core == 0, low, high), jnp.where(core == 0, high, low)], axis=1)
    return jnp.transpose(jnp.broadcast_to(use, (128, length)), (1, 0))


def time_kernel(tps, begin, form, info_ref, first_ref, visible_ref, own_ref, other_ref, *refs):
    weights, outs, kept_ref = refs[:4], refs[4:-1], refs[-1]
    half, d = own_ref.shape[1:]
    step = pl.program_id(0)
    usable = []
    for i in range(tps):
        track = begin + step * tps + i
        usable.append(usable_columns(info_ref[0], first_ref[track], visible_ref[pl.ds(track, 1), :]))
    own = own_ref[...].reshape(tps * half, d).astype(F32)
    other = other_ref[...].reshape(tps * half, d).astype(F32)
    settled = settle(own, other, usable, *weights)
    if form == "tracks":
        outs[0][...] = settled.astype(BF).reshape(tps, half, d)
        return
    spots = outs[0].shape[0]
    rows = half // spots
    last = outs[0].shape[1] // tps
    first = rows - last
    for t in range(spots):
        at = [i * half + t * rows + first for i in range(tps)]
        outs[0][t] = jnp.concatenate([settled[a : a + last] for a in at], axis=0).astype(BF)
    if form == "dense":
        return
    kept_ref[...] = settled
    for k in range(spots):
        t = lax.rem(info_ref[1] + k, spots)
        at = [pl.multiple_of(i * half + t * rows, 8) for i in range(tps)]
        outs[1 + k][...] = jnp.concatenate([kept_ref[pl.ds(a, first), :] for a in at], axis=0).astype(BF)


def full(shape):
    return pl.BlockSpec(shape, lambda *_: (0,) * len(shape))


def time_part(tokens, other, first_frame, visible, info, weights, spots, form, first, begin, count, after):
    _, half, d = tokens.shape
    rows = half // spots
    tps = 4
    if form == "tracks":
        shapes, blocks = [(count, half, d)], [pl.BlockSpec((tps, half, d), lambda i, *_: (i, 0, 0))]
    else:
        last = rows - first
        shapes = [(spots, count * last, d)]
        blocks = [pl.BlockSpec((spots, tps * last, d), lambda i, *_: (0, i, 0))]
    if form == "split":
        shapes += [(count * first, d)] * spots
        blocks += [pl.BlockSpec((tps * first, d), lambda i, *_: (i, 0))] * spots
    total = count * half
    block = pl.BlockSpec((tps, half, d), lambda i, *_: (begin // tps + i, 0, 0))
    kernel = functools.partial(time_kernel, tps, begin, form)
    extra = [] if after is None else [after]
    if extra:
        inner = kernel

        def kernel(info_ref, first_ref, after_ref, *refs):
            inner(info_ref, first_ref, *refs)

    return pl.pallas_call(
        kernel,
        out_shape=[jax.ShapeDtypeStruct(s, BF) for s in shapes],
        grid_spec=pltpu.PrefetchScalarGridSpec(
            num_scalar_prefetch=2,
            grid=(count // tps,),
            in_specs=[pl.BlockSpec(memory_space=pl.ANY)] * len(extra)
            + [full(visible.shape), block, block]
            + [full(w.shape) for w in weights],
            out_specs=blocks,
            scratch_shapes=[pltpu.VMEM((tps * half, d), F32)],
        ),
        compiler_params=pltpu.CompilerParams(vmem_limit_bytes=VMEM),
        cost_estimate=pl.CostEstimate(flops=total * 5_000_000, bytes_accessed=total * d * 4, transcendentals=total * 3600),
        name="time_part",
    )(info, first_frame, *extra, visible, tokens, other, *weights)


def gather_matrix(out_rows, in_rows, source):
    r, c = iota(out_rows, in_rows, 0), iota(out_rows, in_rows, 1)
    return jnp.where(c == source(r), 1.0, 0.0).astype(BF)


class Server:
    def __init__(self, weights):
        init_ref, cq_ref, self.ckv, self.co, self.sqkv, self.so, self.bq, self.bkv, self.bo = weights
        self.init = init_ref[...].astype(F32)
        self.virt, self.d = self.init.shape
        self.lanes = lanes = Lanes(self.d)
        self.tau = lanes.head**-0.5
        vq = normed(dot(normed(self.init).astype(BF), cq_ref[...]), self.tau).astype(BF)
        self.masks = [lanes.heads(self.virt, w) for w in range(2)]
        lane = iota(lanes.width, 2 * self.virt, 1)
        row = iota(lanes.width, 2 * self.virt, 0)
        self.turned_masks, self.value_masks = [], []
        for w in range(2):
            pairs = []
            for h in range(0, HALF, 2):
                start = lanes.first[w] + h * lanes.head + jnp.where(lane < self.virt, 0, lanes.head)
                pairs.append(jnp.where(within(row, start, lanes.head), 1.0, 0.0).astype(BF))
            self.turned_masks.append(pairs)
            sums = iota(self.virt, lanes.width, 1)
            self.value_masks.append(
                [
                    m + jnp.where(within(sums, lanes.sums[w] + 16 * h, 16), 1.0, 0.0).astype(BF)
                    for h, m in enumerate(self.masks[w])
                ]
            )
        self.stacked = [
            jnp.concatenate([lanes.cut(vq, w) * m for m in self.masks[w]], axis=0) for w in range(2)
        ]

    def attend(self, query, key, value, masks):
        lanes, pair = self.lanes, []
        turned = jnp.transpose(jnp.concatenate([key, key], axis=0), (1, 0))
        for w in range(2):
            k = turned[lanes.begin[w] : lanes.begin[w] + lanes.width]
            k = jnp.concatenate([k * m for m in self.turned_masks[w]], axis=1)
            p = jnp.exp(dot(lanes.cut(query, w), k)).astype(BF)
            v = jnp.concatenate([value[w] * m for m in self.value_masks[w]], axis=0)
            pair.append(dot(p, v))
        return pair

    def divide(self, pairs):
        return self.lanes.divide(*[jnp.concatenate([p[w] for p in pairs], axis=0) for w in range(2)])

    def run(self, settled, frames):
        d, lanes, virt = self.d, self.lanes, self.virt
        tracks = settled.shape[0] // frames
        settled_norm = normed(settled).astype(BF)
        crossed = dot(settled_norm, self.ckv[...])
        track_key = normed(crossed[:, :d]).astype(BF)
        track_value = crossed[:, d:]
        track_query = normed(dot(settled_norm, self.bq[...]), self.tau).astype(BF)
        ones = [lanes.with_ones(track_value, w).astype(BF) for w in range(2)]
        pairs = []
        for f in range(frames):
            rows = slice(f * tracks, (f + 1) * tracks)
            pair = []
            turned = jnp.transpose(track_key[rows], (1, 0))
            for w in range(2):
                p = jnp.exp(dot(self.stacked[w], turned[lanes.begin[w] : lanes.begin[w] + lanes.width])).astype(BF)
                pair.append(lanes.choose(dot(p, ones[w][rows]), virt, w))
            pairs.append(pair)
        virtual = jnp.concatenate([self.init] * frames, axis=0) + dot(self.divide(pairs), self.co[...])
        selfed = dot(normed(virtual).astype(BF), self.sqkv[...])
        query = normed(selfed[:, :d], self.tau).astype(BF)
        key = normed(selfed[:, d : 2 * d]).astype(BF)
        value = [lanes.with_ones(selfed[:, 2 * d :], w).astype(BF) for w in range(2)]
        at = [slice(f * virt, (f + 1) * virt) for f in range(frames)]
        mixed = self.divide([self.attend(query[r], key[r], [v[r] for v in value], self.masks) for r in at])
        virtual = virtual + dot(mixed, self.so[...])
        backed = dot(normed(virtual).astype(BF), self.bkv[...])
        key = normed(backed[:, :d]).astype(BF)
        value = [lanes.with_ones(backed[:, d:], w).astype(BF) for w in range(2)]
        masks = [lanes.heads(tracks, w) for w in range(2)]
        mixed = self.divide(
            [
                self.attend(track_query[f * tracks : (f + 1) * tracks], key[r], [v[r] for v in value], masks)
                for f, r in enumerate(at)
            ]
        )
        return (settled + dot(mixed, self.bo[...])).astype(BF)


def rows_kernel(frames, block, group, x_ref, *refs):
    weights, out_ref, rows_ref = refs[:-2], refs[-2], refs[-1]
    total = x_ref.shape[0]
    tracks = total // frames
    part = group // frames
    there = gather_matrix(group, group, lambda r: (r % part) * frames + r // part)
    for g in range(total // group):
        moved = dot(there, x_ref[g * group : (g + 1) * group, :]).astype(BF)
        for f in range(frames):
            rows_ref[f * tracks + g * part : f * tracks + (g + 1) * part, :] = moved[f * part : (f + 1) * part]
    server = Server(weights)

    def body(b, carry):
        at = pl.ds(pl.multiple_of(b * (block * tracks), block * tracks), block * tracks)
        rows_ref[at, :] = server.run(rows_ref[at, :].astype(F32), block)
        return carry

    lax.fori_loop(0, frames // block, body, 0)
    back = gather_matrix(group, group, lambda r: (r % frames) * part + r // frames)
    for g in range(total // group):
        moved = jnp.concatenate(
            [rows_ref[f * tracks + g * part : f * tracks + (g + 1) * part, :] for f in range(frames)], axis=0
        )
        out_ref[g * group : (g + 1) * group, :] = dot(back, moved).astype(BF)


def rows_part(x, frames, weights):
    return pl.pallas_call(
        functools.partial(rows_kernel, frames, min(frames, 4), max(256, 16 * frames)),
        out_shape=jax.ShapeDtypeStruct(x.shape, BF),
        grid=(1,),
        in_specs=[full(a.shape) for a in (x, *weights)],
        out_specs=full(x.shape),
        scratch_shapes=[pltpu.VMEM(x.shape, BF)],
        compiler_params=pltpu.CompilerParams(vmem_limit_bytes=VMEM),
        name="rows_part",
    )(x, *weights)


def frames_kernel(spots, n_out, spans, begins, frames, block, info_ref, dense_ref, *refs):
    n = len(refs) - 10 - n_out
    xs, weights, outs, rows_ref = refs[:n], refs[n : n + 9], refs[n + 9 : -1], refs[-1]
    counts = (dense_ref.shape[1] // spans[0], xs[0].shape[-2] // spans[1])
    both = sum(counts)
    tracks = spots * both
    depth = counts[0] * spans[0] + counts[1] * spans[1]

    def source(r):
        f, track = r // both, r % both
        rest = counts[0] * spans[0] + (track - counts[0]) * spans[1] + begins[1] + f
        return jnp.where(track < counts[0], track * spans[0] + begins[0] + f, rest)

    pick = gather_matrix(frames * both, depth, source)
    for k in range(spots):
        back = lax.rem(info_ref[1] + spots - k, spots)
        rows = jnp.concatenate([dense_ref[back], xs[k][...] if n > 1 else xs[0][back]], axis=0)
        moved = dot(pick, rows).astype(BF)
        for f in range(frames):
            rows_ref[f * tracks + k * both : f * tracks + (k + 1) * both, :] = moved[f * both : (f + 1) * both]
    server = Server(weights)
    for b in range(0, frames, block):
        tracked = server.run(rows_ref[b * tracks : (b + block) * tracks, :].astype(F32), block)
        for f in range(block):
            to = slice((b + f) * both, (b + f + 1) * both)
            for k in range(spots):
                rows = tracked[f * tracks + k * both : f * tracks + (k + 1) * both]
                if len(outs) > 1:
                    outs[k][to, :] = rows
                else:
                    outs[0][lax.rem(info_ref[1] + spots - k, spots), to, :] = rows


def frames_part(dense, xs, info, spans, begins, form, frames, block, weights):
    spots, _, d = dense.shape
    both = dense.shape[1] // spans[0] + xs[0].shape[-2] // spans[1]
    if form == "dense":
        shapes = [(spots, frames * both, d)]
    else:
        shapes = [(frames * both, d)] * spots
    rows = frames * spots * both
    return pl.pallas_call(
        functools.partial(frames_kernel, spots, len(shapes), spans, begins, frames, block),
        out_shape=[jax.ShapeDtypeStruct(s, BF) for s in shapes],
        grid_spec=pltpu.PrefetchScalarGridSpec(
            num_scalar_prefetch=1,
            grid=(1,),
            in_specs=[full(a.shape) for a in (dense, *xs, *weights)],
            out_specs=[full(s) for s in shapes],
            scratch_shapes=[pltpu.VMEM((rows, d), BF)],
        ),
        compiler_params=pltpu.CompilerParams(vmem_limit_bytes=VMEM),
        cost_estimate=pl.CostEstimate(flops=rows * 10_000_000, bytes_accessed=rows * d * 4, transcendentals=rows * 2000),
        name="frames_part",
    )(info, dense, *xs, *weights)


def home_kernel(spots, info_ref, dense_ref, *refs):
    xs, out_ref = refs[:-1], refs[-1]
    tracks, _, d = out_ref.shape
    depth = dense_ref.shape[1] + xs[0].shape[0]
    span = depth // tracks
    pick = gather_matrix(depth, depth, lambda r: (r % span) * tracks + r // span)
    for k in range(spots):
        t = lax.rem(info_ref[1] + k, spots)
        rows = jnp.concatenate([dense_ref[t], xs[k][...]], axis=0)
        at = pl.ds(pl.multiple_of(t * span, span), span)
        out_ref[:, at, :] = dot(pick, rows).astype(BF).reshape(tracks, span, d)


def home(dense, xs, info, tracks):
    spots, _, d = dense.shape
    out = (tracks, spots * (dense.shape[1] + xs[0].shape[0]) // tracks, d)
    return pl.pallas_call(
        functools.partial(home_kernel, spots),
        out_shape=jax.ShapeDtypeStruct(out, BF),
        grid_spec=pltpu.PrefetchScalarGridSpec(
            num_scalar_prefetch=1,
            grid=(1,),
            in_specs=[full(a.shape) for a in (dense, *xs)],
            out_specs=full(out),
        ),
        compiler_params=pltpu.CompilerParams(vmem_limit_bytes=VMEM // 2),
        name="home",
    )(info, dense, *xs)


def exchange(x):
    return lax.all_to_all(x, "tracks", split_axis=0, concat_axis=0, tiled=True)


def swap_cores(x):
    return lax.ppermute(x, "frames", [(0, 1), (1, 0)])


def shift(xs, spots, sign):
    return [xs[0]] + [
        lax.ppermute(xs[k], "tracks", [(i, (i + sign * k) % spots) for i in range(spots)]) for k in range(1, spots)
    ]


def simple(spots, tokens, first_frame, visible, info, time_weights, virtual_weights):
    tracks, half, d = tokens.shape
    rows = half // spots
    (settled,) = time_part(
        tokens, swap_cores(tokens), first_frame, visible, info, time_weights, spots, "tracks", 0, 0, tracks, None
    )
    settled = jnp.transpose(settled.reshape(tracks, spots, rows, d), (1, 0, 2, 3))
    tracked = rows_part(exchange(settled).reshape(-1, d), rows, virtual_weights)
    joined = exchange(tracked.reshape(spots, tracks, rows, d))
    return jnp.transpose(joined, (1, 0, 2, 3)).reshape(tracks, half, d)


def pipelined(spots, tokens, first_frame, visible, info, time_weights, virtual_weights):
    tracks, half, d = tokens.shape
    rows = half // spots
    n, m = FIRST_TRACKS, FIRST_FRAMES
    common = (first_frame, visible, info, time_weights, spots)
    other = swap_cores(tokens)
    (dense,) = time_part(tokens, other, *common, "dense", 0, 0, n, None)
    rest, *first = time_part(tokens, other, *common, "split", m, n, tracks - n, dense)
    dense, first, rest = exchange(dense), shift(first, spots, 1), exchange(rest)
    (first,) = frames_part(dense, first, info, (rows, m), (0, 0), "dense", m, BLOCK, virtual_weights)
    rest = frames_part(dense, [rest], info, (rows, rows - m), (m, 0), "pieces", rows - m, BLOCK, virtual_weights)
    return home(exchange(first), shift(rest, spots, -1), info, tracks)


def per_device(spots, tokens, first_frame, visible, *weights):
    tracks, half, _ = tokens.shape
    rows = half // spots
    fits = tracks % 16 == 0 and rows % 16 == 0 and (rows - FIRST_FRAMES) % 8 == 0 and FIRST_TRACKS < tracks and FIRST_FRAMES < rows
    info = jnp.stack([lax.axis_index("frames"), lax.axis_index("tracks")]).astype(jnp.int32)
    run = pipelined if fits else simple
    return run(spots, tokens, first_frame, visible, info, weights[:4], weights[4:])


FIRST_TRACKS = 8
FIRST_FRAMES = 8
BLOCK = 8


def solution(mesh):
    rows = ("groups", "tracks")
    placed = (P(rows, "frames", None), P(rows), P(rows, None)) + (P(),) * 13
    return jax.shard_map(
        functools.partial(per_device, mesh.shape["tracks"]),
        mesh=mesh,
        in_specs=placed,
        out_specs=P(rows, "frames", None),
        check_vma=False,
    )
```

```python
import functools

import jax
import jax.numpy as jnp
from jax import lax
from jax.experimental import pallas as pl
from jax.experimental.pallas import tpu as pltpu
from jax.sharding import PartitionSpec as P

HEADS = 8
HALF = HEADS // 2
EPS = 1e-06
BF = jnp.bfloat16
F32 = jnp.float32
VMEM = 62 * 1024 * 1024


def dot(a, b):
    return lax.dot_general(a, b, (((1,), (0,)), ((), ())), preferred_element_type=F32)


def dot_t(a, b):
    return lax.dot_general(a, b, (((1,), (1,)), ((), ())), preferred_element_type=F32)


def normed(x, scale=None):
    r = lax.rsqrt(jnp.mean(x * x, axis=-1, keepdims=True) + EPS)
    return x * (r if scale is None else r * scale)


def gelu(x):
    c = 0.7978845608028654
    h = 0.5 * x
    return h + h * jnp.tanh(x * (c + (c * 0.044715) * (x * x)))


def iota(rows, columns, axis):
    return lax.broadcasted_iota(jnp.int32, (rows, columns), axis)


def within(lane, start, count):
    return (lane >= start) & (lane < start + count)


class Lanes:
    def __init__(self, d):
        self.d = d
        self.head = d // HEADS
        self.width = -(-HALF * self.head // 128) * 128
        self.over = 2 * self.width - d
        self.spare = self.width - HALF * self.head
        assert self.spare >= 16 * HALF and self.over == 128 and self.spare <= 64
        self.begin = (0, d - self.width)
        self.first = (0, self.spare)
        self.sums = (HALF * self.head, 0)

    def cut(self, x, w):
        return x[:, self.begin[w] : self.begin[w] + self.width]

    def heads(self, rows, w):
        lane = iota(rows, self.width, 1)
        return [jnp.where(within(lane, self.first[w] + h * self.head, self.head), 1.0, 0.0).astype(BF) for h in range(HALF)]

    def with_ones(self, v, w):
        lane = iota(v.shape[0], self.width, 1)
        return jnp.where(within(lane, self.first[w], HALF * self.head), self.cut(v, w), 1.0)

    def choose(self, o, rows, w):
        lane = iota(rows, self.width, 1)
        out = o[:rows]
        for h in range(1, HALF):
            own = within(lane, self.first[w] + h * self.head, self.head) | within(lane, self.sums[w] + 16 * h, 16)
            out = jnp.where(own, o[h * rows : (h + 1) * rows], out)
        return out

    def divide(self, low, high):
        rows = low.shape[0]
        lane = iota(rows, 128, 1)
        cut = self.width - self.over
        low_part, high_part = low[:, cut:], high[:, : self.over]
        split = self.over - self.spare
        sums = 1.0 / jnp.where(lane < split, high_part, low_part)
        pieces = [low[:, i : i + 128] for i in range(0, cut, 128)]
        pieces.append(jnp.where(lane < split, low_part, high_part))
        pieces += [high[:, i : i + 128] for i in range(self.over, self.width, 128)]
        out = []
        for i, piece in enumerate(pieces):
            head = (lane + 128 * i) // self.head
            spot = jnp.where(head < HALF, self.sums[0] - cut + 16 * head, self.sums[1] + 16 * (head - HALF))
            out.append(piece * jnp.take_along_axis(sums, spot, axis=1))
        return jnp.concatenate(out, axis=1).astype(BF)


def settle(own, other, usable, qkv_ref, out_w_ref, expand_ref, shrink_ref):
    tracks = len(usable)
    d = own.shape[1]
    half = own.shape[0] // tracks
    lanes = Lanes(d)
    own_norm = normed(own).astype(BF)
    query = normed(dot(own_norm, qkv_ref[:, :d]), lanes.head**-0.5).astype(BF)
    both = dot(jnp.concatenate([own_norm, normed(other).astype(BF)], axis=0), qkv_ref[:, d:])
    key = normed(both[:, :d]).astype(BF)
    value = both[:, d:]
    masks = [lanes.heads(half, w) for w in range(2)]
    mixed = []
    def scored(i, w):
        mine = slice(i * half, (i + 1) * half)
        away = slice((tracks + i) * half, (tracks + i + 1) * half)
        k = jnp.concatenate([key[mine], key[away]], axis=0)
        q = lanes.cut(query[mine], w)
        return dot_t(jnp.concatenate([q * m for m in masks[w]], axis=0), lanes.cut(k, w))

    todo = [(i, w) for i in range(tracks) for w in range(2)]
    scores = [scored(*todo[0])]
    pair = []
    for at, (i, w) in enumerate(todo):
        if at + 1 < len(todo):
            scores.append(scored(*todo[at + 1]))
        mine = slice(i * half, (i + 1) * half)
        away = slice((tracks + i) * half, (tracks + i + 1) * half)
        v = jnp.concatenate([value[mine], value[away]], axis=0)
        weights = jnp.exp(scores[at]).astype(BF)
        use = jnp.concatenate([usable[i]] * (lanes.width // 128), axis=1)
        o = dot(weights, (lanes.with_ones(v, w) * use).astype(BF))
        pair.append(lanes.choose(o, half, w))
        if w == 1:
            mixed.append(lanes.divide(*pair))
            pair = []
    middle = own + dot(jnp.concatenate(mixed, axis=0), out_w_ref[...])
    hidden = gelu(dot(normed(middle).astype(BF), expand_ref[...])).astype(BF)
    return middle + dot(hidden, shrink_ref[...])


def usable_columns(core, first, seen):
    length = seen.shape[1]
    frame = iota(1, length, 1)
    use = (frame >= first) & ((seen == 1) | (frame == first))
    use = jnp.where(use, 1.0, 0.0)
    low, high = use[:, : length // 2], use[:, length // 2 :]
    use = jnp.concatenate([jnp.where(core == 0, low, high), jnp.where(core == 0, high, low)], axis=1)
    return jnp.transpose(jnp.broadcast_to(use, (128, length)), (1, 0))


def time_kernel(tps, begin, form, info_ref, first_ref, visible_ref, own_ref, other_ref, *refs):
    weights, outs, kept_ref = refs[:4], refs[4:-1], refs[-1]
    half, d = own_ref.shape[1:]
    step = pl.program_id(0)
    usable = []
    for i in range(tps):
        track = begin + step * tps + i
        usable.append(usable_columns(info_ref[0], first_ref[track], visible_ref[pl.ds(track, 1), :]))
    own = own_ref[...].reshape(tps * half, d).astype(F32)
    other = other_ref[...].reshape(tps * half, d).astype(F32)
    settled = settle(own, other, usable, *weights)
    if form == "tracks":
        outs[0][...] = settled.astype(BF).reshape(tps, half, d)
        return
    spots = outs[0].shape[0]
    rows = half // spots
    last = outs[0].shape[1] // tps
    first = rows - last
    for t in range(spots):
        at = [i * half + t * rows + first for i in range(tps)]
        outs[0][t] = jnp.concatenate([settled[a : a + last] for a in at], axis=0).astype(BF)
    if form == "dense":
        return
    kept_ref[...] = settled
    for k in range(spots):
        t = partner(info_ref[1], k, spots, 1)
        at = [pl.multiple_of(i * half + t * rows, 8) for i in range(tps)]
        outs[1 + k][...] = jnp.concatenate([kept_ref[pl.ds(a, first), :] for a in at], axis=0).astype(BF)


def full(shape):
    return pl.BlockSpec(shape, lambda *_: (0,) * len(shape))


def time_part(tokens, other, first_frame, visible, info, weights, spots, form, first, begin, count, after):
    _, half, d = tokens.shape
    rows = half // spots
    tps = 4
    if form == "tracks":
        shapes, blocks = [(count, half, d)], [pl.BlockSpec((tps, half, d), lambda i, *_: (i, 0, 0))]
    else:
        last = rows - first
        shapes = [(spots, count * last, d)]
        blocks = [pl.BlockSpec((spots, tps * last, d), lambda i, *_: (0, i, 0))]
    if form == "split":
        shapes += [(count * first, d)] * spots
        blocks += [pl.BlockSpec((tps * first, d), lambda i, *_: (i, 0))] * spots
    total = count * half
    block = pl.BlockSpec((tps, half, d), lambda i, *_: (begin // tps + i, 0, 0))
    kernel = functools.partial(time_kernel, tps, begin, form)
    extra = [] if after is None else [after]
    if extra:
        inner = kernel

        def kernel(info_ref, first_ref, after_ref, *refs):
            inner(info_ref, first_ref, *refs)

    return pl.pallas_call(
        kernel,
        out_shape=[jax.ShapeDtypeStruct(s, BF) for s in shapes],
        grid_spec=pltpu.PrefetchScalarGridSpec(
            num_scalar_prefetch=2,
            grid=(count // tps,),
            in_specs=[pl.BlockSpec(memory_space=pl.ANY)] * len(extra)
            + [full(visible.shape), block, block]
            + [full(w.shape) for w in weights],
            out_specs=blocks,
            scratch_shapes=[pltpu.VMEM((tps * half, d), F32)],
        ),
        compiler_params=pltpu.CompilerParams(vmem_limit_bytes=VMEM),
        cost_estimate=pl.CostEstimate(flops=total * 5_000_000, bytes_accessed=total * d * 4, transcendentals=total * 3600),
        name="time_part",
    )(info, first_frame, *extra, visible, tokens, other, *weights)


def partner(spot, k, spots, sign):
    if spots & (spots - 1) == 0:
        return spot ^ k
    return (spot + spots + sign * k) % spots


def gather_matrix(out_rows, in_rows, source):
    r, c = iota(out_rows, in_rows, 0), iota(out_rows, in_rows, 1)
    return jnp.where(c == source(r), 1.0, 0.0).astype(BF)


class Server:
    def __init__(self, weights):
        init_ref, cq_ref, self.ckv, self.co, self.sqkv, self.so, self.bq, self.bkv, self.bo = weights
        self.init = init_ref[...].astype(F32)
        self.virt, self.d = self.init.shape
        self.lanes = lanes = Lanes(self.d)
        self.tau = lanes.head**-0.5
        vq = normed(dot(normed(self.init).astype(BF), cq_ref[...]), self.tau).astype(BF)
        self.masks = [lanes.heads(self.virt, w) for w in range(2)]
        lane = iota(lanes.width, 2 * self.virt, 1)
        row = iota(lanes.width, 2 * self.virt, 0)
        self.turned_masks, self.value_masks = [], []
        for w in range(2):
            pairs = []
            for h in range(0, HALF, 2):
                start = lanes.first[w] + h * lanes.head + jnp.where(lane < self.virt, 0, lanes.head)
                pairs.append(jnp.where(within(row, start, lanes.head), 1.0, 0.0).astype(BF))
            self.turned_masks.append(pairs)
            sums = iota(self.virt, lanes.width, 1)
            self.value_masks.append(
                [
                    m + jnp.where(within(sums, lanes.sums[w] + 16 * h, 16), 1.0, 0.0).astype(BF)
                    for h, m in enumerate(self.masks[w])
                ]
            )
        self.stacked = [
            jnp.concatenate([lanes.cut(vq, w) * m for m in self.masks[w]], axis=0) for w in range(2)
        ]

    def attend(self, query, key, value, masks):
        lanes, pair = self.lanes, []
        turned = jnp.transpose(jnp.concatenate([key, key], axis=0), (1, 0))
        for w in range(2):
            k = turned[lanes.begin[w] : lanes.begin[w] + lanes.width]
            k = jnp.concatenate([k * m for m in self.turned_masks[w]], axis=1)
            p = jnp.exp(dot(lanes.cut(query, w), k)).astype(BF)
            v = jnp.concatenate([value[w] * m for m in self.value_masks[w]], axis=0)
            pair.append(dot(p, v))
        return pair

    def divide(self, pairs):
        return self.lanes.divide(*[jnp.concatenate([p[w] for p in pairs], axis=0) for w in range(2)])

    def run(self, settled, frames):
        d, lanes, virt = self.d, self.lanes, self.virt
        tracks = settled.shape[0] // frames
        settled_norm = normed(settled).astype(BF)
        crossed = dot(settled_norm, self.ckv[...])
        track_key = normed(crossed[:, :d]).astype(BF)
        track_value = crossed[:, d:]
        track_query = normed(dot(settled_norm, self.bq[...]), self.tau).astype(BF)
        ones = [lanes.with_ones(track_value, w).astype(BF) for w in range(2)]
        pairs = []
        for f in range(frames):
            rows = slice(f * tracks, (f + 1) * tracks)
            pair = []
            turned = jnp.transpose(track_key[rows], (1, 0))
            for w in range(2):
                p = jnp.exp(dot(self.stacked[w], turned[lanes.begin[w] : lanes.begin[w] + lanes.width])).astype(BF)
                pair.append(lanes.choose(dot(p, ones[w][rows]), virt, w))
            pairs.append(pair)
        virtual = jnp.concatenate([self.init] * frames, axis=0) + dot(self.divide(pairs), self.co[...])
        selfed = dot(normed(virtual).astype(BF), self.sqkv[...])
        query = normed(selfed[:, :d], self.tau).astype(BF)
        key = normed(selfed[:, d : 2 * d]).astype(BF)
        value = [lanes.with_ones(selfed[:, 2 * d :], w).astype(BF) for w in range(2)]
        at = [slice(f * virt, (f + 1) * virt) for f in range(frames)]
        mixed = self.divide([self.attend(query[r], key[r], [v[r] for v in value], self.masks) for r in at])
        virtual = virtual + dot(mixed, self.so[...])
        backed = dot(normed(virtual).astype(BF), self.bkv[...])
        key = normed(backed[:, :d]).astype(BF)
        value = [lanes.with_ones(backed[:, d:], w).astype(BF) for w in range(2)]
        masks = [lanes.heads(tracks, w) for w in range(2)]
        mixed = self.divide(
            [
                self.attend(track_query[f * tracks : (f + 1) * tracks], key[r], [v[r] for v in value], masks)
                for f, r in enumerate(at)
            ]
        )
        return (settled + dot(mixed, self.bo[...])).astype(BF)


def rows_kernel(frames, block, group, x_ref, *refs):
    weights, out_ref, rows_ref = refs[:-2], refs[-2], refs[-1]
    total = x_ref.shape[0]
    tracks = total // frames
    part = group // frames
    there = gather_matrix(group, group, lambda r: (r % part) * frames + r // part)
    for g in range(total // group):
        moved = dot(there, x_ref[g * group : (g + 1) * group, :]).astype(BF)
        for f in range(frames):
            rows_ref[f * tracks + g * part : f * tracks + (g + 1) * part, :] = moved[f * part : (f + 1) * part]
    server = Server(weights)

    def body(b, carry):
        at = pl.ds(pl.multiple_of(b * (block * tracks), block * tracks), block * tracks)
        rows_ref[at, :] = server.run(rows_ref[at, :].astype(F32), block)
        return carry

    lax.fori_loop(0, frames // block, body, 0)
    back = gather_matrix(group, group, lambda r: (r % frames) * part + r // frames)
    for g in range(total // group):
        moved = jnp.concatenate(
            [rows_ref[f * tracks + g * part : f * tracks + (g + 1) * part, :] for f in range(frames)], axis=0
        )
        out_ref[g * group : (g + 1) * group, :] = dot(back, moved).astype(BF)


def rows_part(x, frames, weights):
    return pl.pallas_call(
        functools.partial(rows_kernel, frames, min(frames, 4), max(256, 16 * frames)),
        out_shape=jax.ShapeDtypeStruct(x.shape, BF),
        grid=(1,),
        in_specs=[full(a.shape) for a in (x, *weights)],
        out_specs=full(x.shape),
        scratch_shapes=[pltpu.VMEM(x.shape, BF)],
        compiler_params=pltpu.CompilerParams(vmem_limit_bytes=VMEM),
        name="rows_part",
    )(x, *weights)


def frames_kernel(spots, n_out, spans, begins, frames, block, info_ref, dense_ref, *refs):
    n = len(refs) - 10 - n_out
    xs, weights, outs, rows_ref = refs[:n], refs[n : n + 9], refs[n + 9 : -1], refs[-1]
    counts = (dense_ref.shape[1] // spans[0], xs[0].shape[-2] // spans[1])
    both = sum(counts)
    tracks = spots * both
    depth = counts[0] * spans[0] + counts[1] * spans[1]

    def source(r):
        f, track = r // both, r % both
        rest = counts[0] * spans[0] + (track - counts[0]) * spans[1] + begins[1] + f
        return jnp.where(track < counts[0], track * spans[0] + begins[0] + f, rest)

    pick = gather_matrix(frames * both, depth, source)
    for k in range(spots):
        back = partner(info_ref[1], k, spots, -1)
        rows = jnp.concatenate([dense_ref[back], xs[k][...] if n > 1 else xs[0][back]], axis=0)
        moved = dot(pick, rows).astype(BF)
        for f in range(frames):
            rows_ref[f * tracks + k * both : f * tracks + (k + 1) * both, :] = moved[f * both : (f + 1) * both]
    server = Server(weights)
    for b in range(0, frames, block):
        tracked = server.run(rows_ref[b * tracks : (b + block) * tracks, :].astype(F32), block)
        for f in range(block):
            to = slice((b + f) * both, (b + f + 1) * both)
            for k in range(spots):
                rows = tracked[f * tracks + k * both : f * tracks + (k + 1) * both]
                if len(outs) > 1:
                    outs[k][to, :] = rows
                else:
                    outs[0][partner(info_ref[1], k, spots, -1), to, :] = rows


def frames_part(dense, xs, info, spans, begins, form, frames, block, weights):
    spots, _, d = dense.shape
    both = dense.shape[1] // spans[0] + xs[0].shape[-2] // spans[1]
    if form == "dense":
        shapes = [(spots, frames * both, d)]
    else:
        shapes = [(frames * both, d)] * spots
    rows = frames * spots * both
    return pl.pallas_call(
        functools.partial(frames_kernel, spots, len(shapes), spans, begins, frames, block),
        out_shape=[jax.ShapeDtypeStruct(s, BF) for s in shapes],
        grid_spec=pltpu.PrefetchScalarGridSpec(
            num_scalar_prefetch=1,
            grid=(1,),
            in_specs=[full(a.shape) for a in (dense, *xs, *weights)],
            out_specs=[full(s) for s in shapes],
            scratch_shapes=[pltpu.VMEM((rows, d), BF)],
        ),
        compiler_params=pltpu.CompilerParams(vmem_limit_bytes=VMEM),
        cost_estimate=pl.CostEstimate(flops=rows * 10_000_000, bytes_accessed=rows * d * 4, transcendentals=rows * 2000),
        name="frames_part",
    )(info, dense, *xs, *weights)


def home_kernel(spots, info_ref, dense_ref, *refs):
    xs, out_ref = refs[:-1], refs[-1]
    tracks, _, d = out_ref.shape
    depth = dense_ref.shape[1] + xs[0].shape[0]
    span = depth // tracks
    pick = gather_matrix(depth, depth, lambda r: (r % span) * tracks + r // span)
    for k in range(spots):
        t = partner(info_ref[1], k, spots, 1)
        rows = jnp.concatenate([dense_ref[t], xs[k][...]], axis=0)
        at = pl.ds(pl.multiple_of(t * span, span), span)
        out_ref[:, at, :] = dot(pick, rows).astype(BF).reshape(tracks, span, d)


def home(dense, xs, info, tracks):
    spots, _, d = dense.shape
    out = (tracks, spots * (dense.shape[1] + xs[0].shape[0]) // tracks, d)
    return pl.pallas_call(
        functools.partial(home_kernel, spots),
        out_shape=jax.ShapeDtypeStruct(out, BF),
        grid_spec=pltpu.PrefetchScalarGridSpec(
            num_scalar_prefetch=1,
            grid=(1,),
            in_specs=[full(a.shape) for a in (dense, *xs)],
            out_specs=full(out),
        ),
        compiler_params=pltpu.CompilerParams(vmem_limit_bytes=VMEM // 2),
        name="home",
    )(info, dense, *xs)


def exchange(x):
    return lax.all_to_all(x, "tracks", split_axis=0, concat_axis=0, tiled=True)


def swap_cores(x):
    return lax.ppermute(x, "frames", [(0, 1), (1, 0)])


def shift(xs, spots, sign):
    out = list(xs)
    for k in [k for p in zip(range(spots // 2, spots), range(spots // 2)) for k in p if k]:
        out[k] = lax.ppermute(xs[k], "tracks", [(i, partner(i, k, spots, sign)) for i in range(spots)])
    return out


def simple(spots, tokens, first_frame, visible, info, time_weights, virtual_weights):
    tracks, half, d = tokens.shape
    rows = half // spots
    (settled,) = time_part(
        tokens, swap_cores(tokens), first_frame, visible, info, time_weights, spots, "tracks", 0, 0, tracks, None
    )
    settled = jnp.transpose(settled.reshape(tracks, spots, rows, d), (1, 0, 2, 3))
    tracked = rows_part(exchange(settled).reshape(-1, d), rows, virtual_weights)
    joined = exchange(tracked.reshape(spots, tracks, rows, d))
    return jnp.transpose(joined, (1, 0, 2, 3)).reshape(tracks, half, d)


def pipelined(spots, tokens, first_frame, visible, info, time_weights, virtual_weights):
    tracks, half, d = tokens.shape
    rows = half // spots
    n, m = FIRST_TRACKS, FIRST_FRAMES
    common = (first_frame, visible, info, time_weights, spots)
    other = swap_cores(tokens)
    (dense,) = time_part(tokens, other, *common, "dense", 0, 0, n, None)
    rest, *first = time_part(tokens, other, *common, "split", m, n, tracks - n, dense)
    dense, first, rest = exchange(dense), shift(first, spots, 1), exchange(rest)
    (first,) = frames_part(dense, first, info, (rows, m), (0, 0), "dense", m, BLOCK, virtual_weights)
    rest = frames_part(dense, [rest], info, (rows, rows - m), (m, 0), "pieces", rows - m, BLOCK, virtual_weights)
    return home(exchange(first), shift(rest, spots, -1), info, tracks)


def per_device(spots, tokens, first_frame, visible, *weights):
    tracks, half, _ = tokens.shape
    rows = half // spots
    fits = tracks % 16 == 0 and rows % 16 == 0 and (rows - FIRST_FRAMES) % 8 == 0 and FIRST_TRACKS < tracks and FIRST_FRAMES < rows
    info = jnp.stack([lax.axis_index("frames"), lax.axis_index("tracks")]).astype(jnp.int32)
    run = pipelined if fits else simple
    return run(spots, tokens, first_frame, visible, info, weights[:4], weights[4:])


FIRST_TRACKS = 8
FIRST_FRAMES = 8
BLOCK = 8


def solution(mesh):
    rows = ("groups", "tracks")
    placed = (P(rows, "frames", None), P(rows), P(rows, None)) + (P(),) * 13
    return jax.shard_map(
        functools.partial(per_device, mesh.shape["tracks"]),
        mesh=mesh,
        in_specs=placed,
        out_specs=P(rows, "frames", None),
        check_vma=False,
    )
```

```python
import functools

import jax
import jax.numpy as jnp
from jax import lax
from jax.experimental import pallas as pl
from jax.experimental.pallas import tpu as pltpu
from jax.sharding import PartitionSpec as P

HEADS = 8
HALF = HEADS // 2
EPS = 1e-06
BF = jnp.bfloat16
F32 = jnp.float32
VMEM = 62 * 1024 * 1024


def dot(a, b):
    return lax.dot_general(a, b, (((1,), (0,)), ((), ())), preferred_element_type=F32)


def dot_t(a, b):
    return lax.dot_general(a, b, (((1,), (1,)), ((), ())), preferred_element_type=F32)


def normed(x, scale=None):
    r = lax.rsqrt(jnp.mean(x * x, axis=-1, keepdims=True) + EPS)
    return x * (r if scale is None else r * scale)


def gelu(x):
    c = 0.7978845608028654
    h = 0.5 * x
    return h + h * jnp.tanh(x * (c + (c * 0.044715) * (x * x)))


def iota(rows, columns, axis):
    return lax.broadcasted_iota(jnp.int32, (rows, columns), axis)


def within(lane, start, count):
    return (lane >= start) & (lane < start + count)


class Lanes:
    def __init__(self, d):
        self.d = d
        self.head = d // HEADS
        self.width = -(-HALF * self.head // 128) * 128
        self.over = 2 * self.width - d
        self.spare = self.width - HALF * self.head
        assert self.spare >= 16 * HALF and self.over == 128 and self.spare <= 64
        self.begin = (0, d - self.width)
        self.first = (0, self.spare)
        self.sums = (HALF * self.head, 0)

    def cut(self, x, w):
        return x[:, self.begin[w] : self.begin[w] + self.width]

    def heads(self, rows, w):
        lane = iota(rows, self.width, 1)
        return [jnp.where(within(lane, self.first[w] + h * self.head, self.head), 1.0, 0.0).astype(BF) for h in range(HALF)]

    def with_ones(self, v, w):
        lane = iota(v.shape[0], self.width, 1)
        return jnp.where(within(lane, self.first[w], HALF * self.head), self.cut(v, w), 1.0)

    def choose(self, o, rows, w):
        lane = iota(rows, self.width, 1)
        out = o[:rows]
        for h in range(1, HALF):
            own = within(lane, self.first[w] + h * self.head, self.head) | within(lane, self.sums[w] + 16 * h, 16)
            out = jnp.where(own, o[h * rows : (h + 1) * rows], out)
        return out

    def divide(self, low, high):
        rows = low.shape[0]
        lane = iota(rows, 128, 1)
        cut = self.width - self.over
        low_part, high_part = low[:, cut:], high[:, : self.over]
        split = self.over - self.spare
        sums = 1.0 / jnp.where(lane < split, high_part, low_part)
        pieces = [low[:, i : i + 128] for i in range(0, cut, 128)]
        pieces.append(jnp.where(lane < split, low_part, high_part))
        pieces += [high[:, i : i + 128] for i in range(self.over, self.width, 128)]
        out = []
        for i, piece in enumerate(pieces):
            head = (lane + 128 * i) // self.head
            spot = jnp.where(head < HALF, self.sums[0] - cut + 16 * head, self.sums[1] + 16 * (head - HALF))
            out.append(piece * jnp.take_along_axis(sums, spot, axis=1))
        return jnp.concatenate(out, axis=1).astype(BF)


def settle(own, other, usable, qkv_ref, out_w_ref, expand_ref, shrink_ref):
    tracks = len(usable)
    d = own.shape[1]
    half = own.shape[0] // tracks
    lanes = Lanes(d)
    own_norm = normed(own).astype(BF)
    query = normed(dot(own_norm, qkv_ref[:, :d]), lanes.head**-0.5).astype(BF)
    both = dot(jnp.concatenate([own_norm, normed(other).astype(BF)], axis=0), qkv_ref[:, d:])
    key = normed(both[:, :d]).astype(BF)
    value = both[:, d:]
    masks = [lanes.heads(half, w) for w in range(2)]
    mixed = []
    def scored(i, w):
        mine = slice(i * half, (i + 1) * half)
        away = slice((tracks + i) * half, (tracks + i + 1) * half)
        k = jnp.concatenate([key[mine], key[away]], axis=0)
        q = lanes.cut(query[mine], w)
        return dot_t(jnp.concatenate([q * m for m in masks[w]], axis=0), lanes.cut(k, w))

    todo = [(i, w) for i in range(tracks) for w in range(2)]
    scores = [scored(*todo[0])]
    pair = []
    for at, (i, w) in enumerate(todo):
        if at + 1 < len(todo):
            scores.append(scored(*todo[at + 1]))
        mine = slice(i * half, (i + 1) * half)
        away = slice((tracks + i) * half, (tracks + i + 1) * half)
        v = jnp.concatenate([value[mine], value[away]], axis=0)
        weights = jnp.exp(scores[at]).astype(BF)
        use = jnp.concatenate([usable[i]] * (lanes.width // 128), axis=1)
        o = dot(weights, (lanes.with_ones(v, w) * use).astype(BF))
        pair.append(lanes.choose(o, half, w))
        if w == 1:
            mixed.append(lanes.divide(*pair))
            pair = []
    middle = own + dot(jnp.concatenate(mixed, axis=0), out_w_ref[...])
    hidden = gelu(dot(normed(middle).astype(BF), expand_ref[...])).astype(BF)
    return middle + dot(hidden, shrink_ref[...])


def usable_columns(core, first, seen):
    length = seen.shape[1]
    frame = iota(1, length, 1)
    use = (frame >= first) & ((seen == 1) | (frame == first))
    use = jnp.where(use, 1.0, 0.0)
    low, high = use[:, : length // 2], use[:, length // 2 :]
    use = jnp.concatenate([jnp.where(core == 0, low, high), jnp.where(core == 0, high, low)], axis=1)
    return jnp.transpose(jnp.broadcast_to(use, (128, length)), (1, 0))


def time_kernel(tps, begin, form, info_ref, first_ref, visible_ref, own_ref, other_ref, *refs):
    weights, outs, kept_ref = refs[:4], refs[4:-1], refs[-1]
    half, d = own_ref.shape[1:]
    step = pl.program_id(0)
    usable = []
    for i in range(tps):
        track = begin + step * tps + i
        usable.append(usable_columns(info_ref[0], first_ref[track], visible_ref[pl.ds(track, 1), :]))
    own = own_ref[...].reshape(tps * half, d).astype(F32)
    other = other_ref[...].reshape(tps * half, d).astype(F32)
    settled = settle(own, other, usable, *weights)
    if form == "tracks":
        outs[0][...] = settled.astype(BF).reshape(tps, half, d)
        return
    spots = outs[0].shape[0]
    rows = half // spots
    last = outs[0].shape[1] // tps
    first = rows - last
    for t in range(spots):
        at = [i * half + t * rows + first for i in range(tps)]
        outs[0][t] = jnp.concatenate([settled[a : a + last] for a in at], axis=0).astype(BF)
    if form == "dense":
        return
    kept_ref[...] = settled
    for k in range(spots):
        t = partner(info_ref[1], k, spots, 1)
        at = [pl.multiple_of(i * half + t * rows, 8) for i in range(tps)]
        outs[1 + k][...] = jnp.concatenate([kept_ref[pl.ds(a, first), :] for a in at], axis=0).astype(BF)


def full(shape):
    return pl.BlockSpec(shape, lambda *_: (0,) * len(shape))


def time_part(tokens, other, first_frame, visible, info, weights, spots, form, first, begin, count, after):
    _, half, d = tokens.shape
    rows = half // spots
    tps = 8 if form == "dense" and count % 8 == 0 else 4
    if form == "tracks":
        shapes, blocks = [(count, half, d)], [pl.BlockSpec((tps, half, d), lambda i, *_: (i, 0, 0))]
    else:
        last = rows - first
        shapes = [(spots, count * last, d)]
        blocks = [pl.BlockSpec((spots, tps * last, d), lambda i, *_: (0, i, 0))]
    if form == "split":
        shapes += [(count * first, d)] * spots
        blocks += [pl.BlockSpec((tps * first, d), lambda i, *_: (i, 0))] * spots
    total = count * half
    block = pl.BlockSpec((tps, half, d), lambda i, *_: (begin // tps + i, 0, 0))
    kernel = functools.partial(time_kernel, tps, begin, form)
    extra = [] if after is None else [after]
    if extra:
        inner = kernel

        def kernel(info_ref, first_ref, after_ref, *refs):
            inner(info_ref, first_ref, *refs)

    return pl.pallas_call(
        kernel,
        out_shape=[jax.ShapeDtypeStruct(s, BF) for s in shapes],
        grid_spec=pltpu.PrefetchScalarGridSpec(
            num_scalar_prefetch=2,
            grid=(count // tps,),
            in_specs=[pl.BlockSpec(memory_space=pl.ANY)] * len(extra)
            + [full(visible.shape), block, block]
            + [full(w.shape) for w in weights],
            out_specs=blocks,
            scratch_shapes=[pltpu.VMEM((tps * half, d), F32)],
        ),
        compiler_params=pltpu.CompilerParams(vmem_limit_bytes=VMEM),
        cost_estimate=pl.CostEstimate(flops=total * 5_000_000, bytes_accessed=total * d * 4, transcendentals=total * 3600),
        name="time_part",
    )(info, first_frame, *extra, visible, tokens, other, *weights)


def partner(spot, k, spots, sign):
    if spots & (spots - 1) == 0:
        return spot ^ k
    return (spot + spots + sign * k) % spots


def gather_matrix(out_rows, in_rows, source):
    r, c = iota(out_rows, in_rows, 0), iota(out_rows, in_rows, 1)
    return jnp.where(c == source(r), 1.0, 0.0).astype(BF)


class Server:
    def __init__(self, weights):
        init_ref, cq_ref, self.ckv, self.co, self.sqkv, self.so, self.bq, self.bkv, self.bo = weights
        self.init = init_ref[...].astype(F32)
        self.virt, self.d = self.init.shape
        self.lanes = lanes = Lanes(self.d)
        self.tau = lanes.head**-0.5
        vq = normed(dot(normed(self.init).astype(BF), cq_ref[...]), self.tau).astype(BF)
        self.masks = [lanes.heads(self.virt, w) for w in range(2)]
        lane = iota(lanes.width, 2 * self.virt, 1)
        row = iota(lanes.width, 2 * self.virt, 0)
        self.turned_masks, self.value_masks = [], []
        for w in range(2):
            pairs = []
            for h in range(0, HALF, 2):
                start = lanes.first[w] + h * lanes.head + jnp.where(lane < self.virt, 0, lanes.head)
                pairs.append(jnp.where(within(row, start, lanes.head), 1.0, 0.0).astype(BF))
            self.turned_masks.append(pairs)
            sums = iota(self.virt, lanes.width, 1)
            self.value_masks.append(
                [
                    m + jnp.where(within(sums, lanes.sums[w] + 16 * h, 16), 1.0, 0.0).astype(BF)
                    for h, m in enumerate(self.masks[w])
                ]
            )
        self.stacked = [
            jnp.concatenate([lanes.cut(vq, w) * m for m in self.masks[w]], axis=0) for w in range(2)
        ]

    def attend(self, query, key, value, masks):
        lanes, pair = self.lanes, []
        turned = jnp.transpose(jnp.concatenate([key, key], axis=0), (1, 0))
        for w in range(2):
            k = turned[lanes.begin[w] : lanes.begin[w] + lanes.width]
            k = jnp.concatenate([k * m for m in self.turned_masks[w]], axis=1)
            p = jnp.exp(dot(lanes.cut(query, w), k)).astype(BF)
            v = jnp.concatenate([value[w] * m for m in self.value_masks[w]], axis=0)
            pair.append(dot(p, v))
        return pair

    def divide(self, pairs):
        return self.lanes.divide(*[jnp.concatenate([p[w] for p in pairs], axis=0) for w in range(2)])

    def run(self, settled, frames):
        d, lanes, virt = self.d, self.lanes, self.virt
        tracks = settled.shape[0] // frames
        settled_norm = normed(settled).astype(BF)
        crossed = dot(settled_norm, self.ckv[...])
        track_key = normed(crossed[:, :d]).astype(BF)
        track_value = crossed[:, d:]
        track_query = normed(dot(settled_norm, self.bq[...]), self.tau).astype(BF)
        ones = [lanes.with_ones(track_value, w).astype(BF) for w in range(2)]
        pairs = []
        for f in range(frames):
            rows = slice(f * tracks, (f + 1) * tracks)
            pair = []
            turned = jnp.transpose(track_key[rows], (1, 0))
            for w in range(2):
                p = jnp.exp(dot(self.stacked[w], turned[lanes.begin[w] : lanes.begin[w] + lanes.width])).astype(BF)
                pair.append(lanes.choose(dot(p, ones[w][rows]), virt, w))
            pairs.append(pair)
        virtual = jnp.concatenate([self.init] * frames, axis=0) + dot(self.divide(pairs), self.co[...])
        selfed = dot(normed(virtual).astype(BF), self.sqkv[...])
        query = normed(selfed[:, :d], self.tau).astype(BF)
        key = normed(selfed[:, d : 2 * d]).astype(BF)
        value = [lanes.with_ones(selfed[:, 2 * d :], w).astype(BF) for w in range(2)]
        at = [slice(f * virt, (f + 1) * virt) for f in range(frames)]
        mixed = self.divide([self.attend(query[r], key[r], [v[r] for v in value], self.masks) for r in at])
        virtual = virtual + dot(mixed, self.so[...])
        backed = dot(normed(virtual).astype(BF), self.bkv[...])
        key = normed(backed[:, :d]).astype(BF)
        value = [lanes.with_ones(backed[:, d:], w).astype(BF) for w in range(2)]
        masks = [lanes.heads(tracks, w) for w in range(2)]
        mixed = self.divide(
            [
                self.attend(track_query[f * tracks : (f + 1) * tracks], key[r], [v[r] for v in value], masks)
                for f, r in enumerate(at)
            ]
        )
        return (settled + dot(mixed, self.bo[...])).astype(BF)


def rows_kernel(frames, block, group, x_ref, *refs):
    weights, out_ref, rows_ref = refs[:-2], refs[-2], refs[-1]
    total = x_ref.shape[0]
    tracks = total // frames
    part = group // frames
    there = gather_matrix(group, group, lambda r: (r % part) * frames + r // part)
    for g in range(total // group):
        moved = dot(there, x_ref[g * group : (g + 1) * group, :]).astype(BF)
        for f in range(frames):
            rows_ref[f * tracks + g * part : f * tracks + (g + 1) * part, :] = moved[f * part : (f + 1) * part]
    server = Server(weights)

    def body(b, carry):
        at = pl.ds(pl.multiple_of(b * (block * tracks), block * tracks), block * tracks)
        rows_ref[at, :] = server.run(rows_ref[at, :].astype(F32), block)
        return carry

    lax.fori_loop(0, frames // block, body, 0)
    back = gather_matrix(group, group, lambda r: (r % frames) * part + r // frames)
    for g in range(total // group):
        moved = jnp.concatenate(
            [rows_ref[f * tracks + g * part : f * tracks + (g + 1) * part, :] for f in range(frames)], axis=0
        )
        out_ref[g * group : (g + 1) * group, :] = dot(back, moved).astype(BF)


def rows_part(x, frames, weights):
    return pl.pallas_call(
        functools.partial(rows_kernel, frames, min(frames, 4), max(256, 16 * frames)),
        out_shape=jax.ShapeDtypeStruct(x.shape, BF),
        grid=(1,),
        in_specs=[full(a.shape) for a in (x, *weights)],
        out_specs=full(x.shape),
        scratch_shapes=[pltpu.VMEM(x.shape, BF)],
        compiler_params=pltpu.CompilerParams(vmem_limit_bytes=VMEM),
        name="rows_part",
    )(x, *weights)


def frames_kernel(spots, n_out, spans, begins, frames, block, info_ref, dense_ref, *refs):
    n = len(refs) - 10 - n_out
    xs, weights, outs, rows_ref = refs[:n], refs[n : n + 9], refs[n + 9 : -1], refs[-1]
    counts = (dense_ref.shape[1] // spans[0], xs[0].shape[-2] // spans[1])
    both = sum(counts)
    tracks = spots * both
    depth = counts[0] * spans[0] + counts[1] * spans[1]

    def source(r):
        f, track = r // both, r % both
        rest = counts[0] * spans[0] + (track - counts[0]) * spans[1] + begins[1] + f
        return jnp.where(track < counts[0], track * spans[0] + begins[0] + f, rest)

    pick = gather_matrix(frames * both, depth, source)
    for k in range(spots):
        back = partner(info_ref[1], k, spots, -1)
        rows = jnp.concatenate([dense_ref[back], xs[k][...] if n > 1 else xs[0][back]], axis=0)
        moved = dot(pick, rows).astype(BF)
        for f in range(frames):
            rows_ref[f * tracks + k * both : f * tracks + (k + 1) * both, :] = moved[f * both : (f + 1) * both]
    server = Server(weights)
    for b in range(0, frames, block):
        tracked = server.run(rows_ref[b * tracks : (b + block) * tracks, :].astype(F32), block)
        for f in range(block):
            to = slice((b + f) * both, (b + f + 1) * both)
            for k in range(spots):
                rows = tracked[f * tracks + k * both : f * tracks + (k + 1) * both]
                if len(outs) > 1:
                    outs[k][to, :] = rows
                else:
                    outs[0][partner(info_ref[1], k, spots, -1), to, :] = rows


def frames_part(dense, xs, info, spans, begins, form, frames, block, weights):
    spots, _, d = dense.shape
    both = dense.shape[1] // spans[0] + xs[0].shape[-2] // spans[1]
    if form == "dense":
        shapes = [(spots, frames * both, d)]
    else:
        shapes = [(frames * both, d)] * spots
    rows = frames * spots * both
    return pl.pallas_call(
        functools.partial(frames_kernel, spots, len(shapes), spans, begins, frames, block),
        out_shape=[jax.ShapeDtypeStruct(s, BF) for s in shapes],
        grid_spec=pltpu.PrefetchScalarGridSpec(
            num_scalar_prefetch=1,
            grid=(1,),
            in_specs=[full(a.shape) for a in (dense, *xs, *weights)],
            out_specs=[full(s) for s in shapes],
            scratch_shapes=[pltpu.VMEM((rows, d), BF)],
        ),
        compiler_params=pltpu.CompilerParams(vmem_limit_bytes=VMEM),
        cost_estimate=pl.CostEstimate(flops=rows * 10_000_000, bytes_accessed=rows * d * 4, transcendentals=rows * 2000),
        name="frames_part",
    )(info, dense, *xs, *weights)


def home_kernel(spots, info_ref, dense_ref, *refs):
    xs, out_ref = refs[:-1], refs[-1]
    tracks, _, d = out_ref.shape
    depth = dense_ref.shape[1] + xs[0].shape[0]
    span = depth // tracks
    pick = gather_matrix(depth, depth, lambda r: (r % span) * tracks + r // span)
    for k in range(spots):
        t = partner(info_ref[1], k, spots, 1)
        rows = jnp.concatenate([dense_ref[t], xs[k][...]], axis=0)
        at = pl.ds(pl.multiple_of(t * span, span), span)
        out_ref[:, at, :] = dot(pick, rows).astype(BF).reshape(tracks, span, d)


def home(dense, xs, info, tracks):
    spots, _, d = dense.shape
    out = (tracks, spots * (dense.shape[1] + xs[0].shape[0]) // tracks, d)
    return pl.pallas_call(
        functools.partial(home_kernel, spots),
        out_shape=jax.ShapeDtypeStruct(out, BF),
        grid_spec=pltpu.PrefetchScalarGridSpec(
            num_scalar_prefetch=1,
            grid=(1,),
            in_specs=[full(a.shape) for a in (dense, *xs)],
            out_specs=full(out),
        ),
        compiler_params=pltpu.CompilerParams(vmem_limit_bytes=VMEM // 2),
        name="home",
    )(info, dense, *xs)


def exchange(x):
    return lax.all_to_all(x, "tracks", split_axis=0, concat_axis=0, tiled=True)


def swap_cores(x):
    return lax.ppermute(x, "frames", [(0, 1), (1, 0)])


def shift(xs, spots, sign):
    out = list(xs)
    for k in [k for p in zip(range(spots // 2, spots), range(spots // 2)) for k in p if k]:
        out[k] = lax.ppermute(xs[k], "tracks", [(i, partner(i, k, spots, sign)) for i in range(spots)])
    return out


def simple(spots, tokens, first_frame, visible, info, time_weights, virtual_weights):
    tracks, half, d = tokens.shape
    rows = half // spots
    (settled,) = time_part(
        tokens, swap_cores(tokens), first_frame, visible, info, time_weights, spots, "tracks", 0, 0, tracks, None
    )
    settled = jnp.transpose(settled.reshape(tracks, spots, rows, d), (1, 0, 2, 3))
    tracked = rows_part(exchange(settled).reshape(-1, d), rows, virtual_weights)
    joined = exchange(tracked.reshape(spots, tracks, rows, d))
    return jnp.transpose(joined, (1, 0, 2, 3)).reshape(tracks, half, d)


def pipelined(spots, tokens, first_frame, visible, info, time_weights, virtual_weights):
    tracks, half, d = tokens.shape
    rows = half // spots
    n, m = FIRST_TRACKS, FIRST_FRAMES
    common = (first_frame, visible, info, time_weights, spots)
    other = swap_cores(tokens)
    (dense,) = time_part(tokens, other, *common, "dense", 0, 0, n, None)
    rest, *first = time_part(tokens, other, *common, "split", m, n, tracks - n, dense)
    dense, first, rest = exchange(dense), shift(first, spots, 1), exchange(rest)
    (first,) = frames_part(dense, first, info, (rows, m), (0, 0), "dense", m, BLOCK, virtual_weights)
    rest = frames_part(dense, [rest], info, (rows, rows - m), (m, 0), "pieces", rows - m, BLOCK, virtual_weights)
    return home(exchange(first), shift(rest, spots, -1), info, tracks)


def per_device(spots, tokens, first_frame, visible, *weights):
    tracks, half, _ = tokens.shape
    rows = half // spots
    fits = tracks % 16 == 0 and rows % 16 == 0 and (rows - FIRST_FRAMES) % 8 == 0 and FIRST_TRACKS < tracks and FIRST_FRAMES < rows
    info = jnp.stack([lax.axis_index("frames"), lax.axis_index("tracks")]).astype(jnp.int32)
    run = pipelined if fits else simple
    return run(spots, tokens, first_frame, visible, info, weights[:4], weights[4:])


FIRST_TRACKS = 8
FIRST_FRAMES = 8
BLOCK = 8


def solution(mesh):
    rows = ("groups", "tracks")
    placed = (P(rows, "frames", None), P(rows), P(rows, None)) + (P(),) * 13
    return jax.shard_map(
        functools.partial(per_device, mesh.shape["tracks"]),
        mesh=mesh,
        in_specs=placed,
        out_specs=P(rows, "frames", None),
        check_vma=False,
    )
```
